128 devices in a mesh: shot: 16 (over z, x), rcv: 8 (over y, core).
Axes of the slice: x: 4, y: 4, z: 4, core: 2. Of those that a mesh axis runs over, the one named last changes fastest.
Arguments:
- traces: bfloat16 [65536, 2000], P(('shot', 'rcv')), may hold values from -6 to 6
- cmp_bin: int32 [65536], P(('shot', 'rcv')), may hold values from 0 to 4095, as said below
- shot_index: int32 [65536], P(('shot', 'rcv')), may hold values from 0 to 2047, as said below
- rcv_index: int32 [65536], P(('shot', 'rcv')), may hold values from 0 to 2047, as said below
- live: int32 [65536], P(('shot', 'rcv')), may hold values 0 or 1
Outputs:
- shot_phase: float32 [2, 2048, 384], P(None, 'shot')
- rcv_phase: float32 [2, 2048, 384], P(None, 'rcv')
The draws below stay inside these ranges and needn't reach their ends.
Inputs may be any that keep to these rules, and one draw needn't show every extreme that they name: `shot_index`: every trace held by the devices of shot-axis index i belongs to one of the shots i * 128 to (i + 1) * 128 - 1. `rcv_index`: every trace held by the devices of rcv-axis index j belongs to one of the receiver channels j * 256 to (j + 1) * 256 - 1. `cmp_bin`: A trace's CMP bin is near the midpoint of its shot's and its receiver's positions along the line; the receiver channels of one rcv index are alternated with those of the others along the whole line.
All inputs are finite; a program needn't handle non-finite values. No bound on the sum of `live` on one device may be relied on, other than what follows from the above.
Results may differ from the reference program's by a relative error of at most 0.0052.
Values may be sent and summed in bfloat16 or wider, within the bound.
A program may use at most 128 MiB of HBM per device.

```python
import math
import jax
import jax.numpy as jnp
from jax import lax

NT = 2000
NF = 384
FLO = 20
SWEEPS = 2
SHOT_DEV = 128
RCV_DEV = 256
TR_DEV = 512
NS = 2048
NR = 2048
NB = 4096
TRACES = 65536
N_RCV = 8


def geometry(key):
    position = jnp.arange(TRACES, dtype=jnp.int32)
    device = position // TR_DEV
    shot_block = device // N_RCV
    rcv_block = device % N_RCV
    shot_offset = jax.random.randint(jax.random.fold_in(key, 101), (TRACES,), 0, SHOT_DEV, dtype=jnp.int32)
    rcv_offset = jax.random.randint(jax.random.fold_in(key, 102), (TRACES,), 0, RCV_DEV, dtype=jnp.int32)
    shots = (shot_block * SHOT_DEV + shot_offset).astype(jnp.int32)
    receivers = (rcv_block * RCV_DEV + rcv_offset).astype(jnp.int32)
    return (shots, receivers)


def draw_shot_index(key, part):
    shots, receivers = geometry(key)
    return shots


def draw_rcv_index(key, part):
    shots, receivers = geometry(key)
    return receivers


def draw_cmp_bin(key, part):
    shots, receivers = geometry(key)
    key = jax.random.fold_in(key, 37)
    rcv_position = receivers % RCV_DEV * N_RCV + receivers // RCV_DEV
    shot_place = shots * NB // NS
    rcv_place = rcv_position * NB // NR
    middle = (shot_place + rcv_place) // 2
    jitter = jax.random.randint(key, (TRACES,), -2, 3, dtype=jnp.int32)
    return jnp.clip(middle + jitter, 0, NB - 1).astype(jnp.int32)


def place_ends(result, stream_key, low, largest):
    place = [jax.random.randint(jax.random.fold_in(stream_key, axis), (), 0, length) for axis, length in enumerate(result.shape)]
    longest = result.shape.index(max(result.shape))
    neighbour = place[:longest] + [(place[longest] + 1) % result.shape[longest]] + place[longest + 1:]
    return result.at[tuple(place)].set(low).at[tuple(neighbour)].set(largest)


def level_of(rng, extent, pieces, least, largest):
    loudness, own = 1.0, jax.random.fold_in(rng, 6)
    for axis_at, blocks in pieces:
        steps = jnp.exp(jax.random.uniform(jax.random.fold_in(own, axis_at), (blocks,), jnp.float32, least / len(pieces), largest / len(pieces)))
        loudness = loudness * jnp.repeat(steps, extent[axis_at] // blocks).reshape([-1 if axis == axis_at else 1 for axis in range(len(extent))])
    return loudness


def bell_draw(stream_key, extent, width, reach, split=(), held_as=jnp.bfloat16):
    level = level_of(stream_key, extent, split, -0.22, 0.18) if split else 1.0
    result = jax.random.normal(stream_key, extent, jnp.float32) * width * level
    return jnp.minimum(jnp.maximum(result, -reach), reach).astype(held_as)


def setup_inputs(seed: int = 0) -> dict:
    streams_of = jax.random.split(jax.random.key(seed), 6)
    return {
        "traces": bell_draw(streams_of[0], (TRACES, NT), 1.0, 6.0, ((0, 128),)),
        "cmp_bin": draw_cmp_bin(jax.random.fold_in(streams_of[5], 71), 0),
        "shot_index": draw_shot_index(jax.random.fold_in(streams_of[5], 71), 0),
        "rcv_index": draw_rcv_index(jax.random.fold_in(streams_of[5], 71), 0),
        "live": place_ends((jax.random.randint(streams_of[4], (TRACES,), 0, 5) < 4).astype(jnp.int32), jax.random.fold_in(streams_of[4], 1), 0, 1),
    }


def dft_table():
    sample = jnp.arange(NT, dtype=jnp.int32)
    band = FLO + jnp.arange(NF, dtype=jnp.int32)
    product = sample[:, None] * band[None, :] % NT
    angles = product.astype(jnp.float32) * (2.0 * math.pi / NT)
    factor = 1.0 / math.sqrt(NT)
    return jnp.concatenate([jnp.cos(angles) * factor, -jnp.sin(angles) * factor], axis=1).astype(jnp.bfloat16)

def normalize_stack(stack):
    band_power = lax.optimization_barrier(jnp.sum(stack * stack, axis=1)) / NF
    return (stack / jnp.sqrt(band_power + 1e-06)[:, None]).astype(jnp.bfloat16)

def soften(real_part, imag_part):
    divisor = jnp.sqrt(real_part * real_part + imag_part * imag_part + 1.0)
    return (real_part / divisor, imag_part / divisor)

def reference(traces, cmp_bin, shot_index, rcv_index, live):
    spectra = jnp.dot(traces, dft_table(), preferred_element_type=jnp.float32).astype(jnp.bfloat16)
    live_w = live.astype(jnp.float32)
    spec_f = spectra.astype(jnp.float32)
    stack = jax.ops.segment_sum(spec_f * live_w[:, None], cmp_bin, num_segments=NB)
    pilot = normalize_stack(stack)
    pilot_rows = jnp.take(pilot, cmp_bin, axis=0).astype(jnp.float32)
    spec_re, spec_im = (spec_f[:, :NF], spec_f[:, NF:])
    pil_re, pil_im = (pilot_rows[:, :NF], pilot_rows[:, NF:])
    cross_re = live_w[:, None] * (spec_re * pil_re + spec_im * pil_im)
    cross_im = live_w[:, None] * (spec_im * pil_re - spec_re * pil_im)
    shot_re = jnp.ones((NS, NF), jnp.float32)
    shot_im = jnp.zeros((NS, NF), jnp.float32)
    rcv_re = jnp.ones((NR, NF), jnp.float32)
    rcv_im = jnp.zeros((NR, NF), jnp.float32)
    for sweep_step in range(SWEEPS):
        at_rcv_re = jnp.take(rcv_re, rcv_index, axis=0)
        at_rcv_im = jnp.take(rcv_im, rcv_index, axis=0)
        at_shot_re = jnp.take(shot_re, shot_index, axis=0)
        at_shot_im = jnp.take(shot_im, shot_index, axis=0)
        zs_re = jax.ops.segment_sum(cross_re * at_rcv_re + cross_im * at_rcv_im, shot_index, num_segments=NS)
        zs_im = jax.ops.segment_sum(cross_im * at_rcv_re - cross_re * at_rcv_im, shot_index, num_segments=NS)
        zr_re = jax.ops.segment_sum(cross_re * at_shot_re + cross_im * at_shot_im, rcv_index, num_segments=NR)
        zr_im = jax.ops.segment_sum(cross_im * at_shot_re - cross_re * at_shot_im, rcv_index, num_segments=NR)
        shot_re, shot_im = soften(zs_re, zs_im)
        rcv_re, rcv_im = soften(zr_re, zr_im)
    return (jnp.stack([shot_re, shot_im]), jnp.stack([rcv_re, rcv_im]))
```

```python
import functools
import math

import jax
import jax.numpy as jnp
import numpy as np
from jax import lax
from jax.experimental import pallas as pl
from jax.experimental.pallas import tpu as pltpu
from jax.sharding import PartitionSpec as P

NT = 2000
NF = 384
FLO = 20
SHOT_DEV = 128
RCV_DEV = 256
TR = 512
NB = 4096
HC = NF
MESH = pl.DeviceIdType.MESH
ORDER = ((0, 1, 2), (1, 2, 0), (2, 0, 1))
BF = jnp.bfloat16
F32 = jnp.float32


def dft_halves():
    sample = np.arange(NT, dtype=np.int32)
    band = FLO + np.arange(NF, dtype=np.int32)
    angles = (sample[:, None] * band[None, :] % NT).astype(np.float32) * np.float32(2.0 * math.pi / NT)
    factor = np.float32(1.0 / math.sqrt(NT))
    re = (np.cos(angles) * factor).reshape(NT, 2, 3, 1, 64)
    im = (-np.sin(angles) * factor).reshape(NT, 2, 3, 1, 64)
    table = np.concatenate([re, im], axis=3).reshape(NT, 2, HC)
    return np.ascontiguousarray(table.transpose(1, 0, 2)).astype(jnp.bfloat16)


def dot(a, b):
    return jnp.dot(a, b, preferred_element_type=F32)


def swap(v):
    return pltpu.roll(v, 64, axis=1)


def low_half(rows):
    return lax.broadcasted_iota(jnp.int32, (rows, 128), 1) < 64


def times_conj(a, b, low):
    same = a * b
    cross = a * swap(b)
    return jnp.where(low, same + swap(same), cross - swap(cross))


def soften(v):
    sq = v * v
    return v * lax.rsqrt(sq + swap(sq) + 1.0)


def kernel(traces, table, idx, shot_out, rcv_out, spec, idxs, oh, oht, part, pilot, cross, psum, shot_one, rcv_one,
           zs_st, zr_st, zs_rv, zr_rv, shot_ph, rcv_ph, shot_all, rcv_all,
           opp1, opp2, opp3, dir1, dir2, dir3, core_s, core_r, rs_s, rs_r, ag_s, ag_r, js_s, js_r, jr_s, jr_r):
    i = lax.axis_index("shot")
    j = lax.axis_index("rcv")
    z, x = lax.div(i, 4), lax.rem(i, 4)
    y, c = lax.div(j, 2), lax.rem(j, 2)
    coord = (x, y, z)
    oc = 1 - c
    partner = (i, 2 * y + oc)

    def at_axis(d, v):
        if d == 0:
            return (z * 4 + v, j)
        if d == 1:
            return (i, 2 * v + c)
        return (v * 4 + x, j)

    plane = [(lax.rem(i + k, 16), j) for k in range(1, 16)]
    line = [at_axis(1, lax.rem(y + k, 4)) for k in range(1, 4)]
    barrier = pltpu.get_barrier_semaphore()
    for dev in plane + line + [partner]:
        pl.semaphore_signal(barrier, inc=1, device_id=dev, device_id_type=MESH)
    pl.semaphore_wait(barrier, 19)

    started = []

    def send(src, dst, s_sem, r_sem, dev):
        copy = pltpu.make_async_remote_copy(src_ref=src, dst_ref=dst, send_sem=s_sem, recv_sem=r_sem, device_id=dev,
                                            device_id_type=MESH)
        copy.start()
        started.append(copy)
        return copy

    idxs[c] = idx[...]
    idx_copy = send(idx, idxs.at[c], core_s.at[0], core_r.at[0], partner)

    def dft(half, dst):
        @pl.loop(0, 4)
        def _(k):
            rows = pl.ds(pl.multiple_of(k * 128, 128), 128)
            dst[rows] = dot(traces[rows, :], table[half]).astype(BF)

    dft(oc, zr_st)
    spec_copy = send(zr_st, spec.at[c], core_s.at[1], core_r.at[1], partner)
    dft(c, spec.at[c])
    idx_copy.wait_recv()

    bin_row = jnp.concatenate([idxs[0, 0:1, :], idxs[1, 0:1, :]], axis=1)

    @pl.loop(0, NB // 128)
    def _(k):
        bins = lax.broadcasted_iota(jnp.int32, (128, 2 * TR), 0) + k * 128
        oh[pl.ds(pl.multiple_of(k * 128, 128), 128)] = jnp.where(bins == bin_row, 1.0, 0.0).astype(BF)

    spec_copy.wait_recv()
    spec_copy.wait_send()

    @pl.loop(0, 16)
    def _(k):
        a = oh[pl.ds(pl.multiple_of(k * 256, 256), 256)]
        r = lax.div(k, 4)
        q3 = lax.rem(k, 4)
        v = (dot(a[:, :TR], spec[0]) + dot(a[:, TR:], spec[1])).astype(BF)
        for s in range(3):
            part[s, r, q3] = v[:, 128 * s:128 * (s + 1)].reshape(4, 4, 16, 128)

    def where(s, r0, fixed):
        return (s, pl.ds(r0, 2)) + tuple(fixed[d] if d in fixed else slice(None) for d in (2, 1, 0))

    opp, direct = (opp1, opp2, opp3), (dir1, dir2, dir3)
    rs = {}

    def fixed_of(s, level):
        return {d: coord[d] for d in ORDER[s][:level]}

    def rs_send(s, level):
        d = ORDER[s][level]
        p = coord[d]
        fixed = fixed_of(s, level)
        plus, minus, far = lax.rem(p + 1, 4), lax.rem(p + 3, 4), lax.rem(p + 2, 4)
        to_plus, to_minus = at_axis(d, plus), at_axis(d, minus)
        o, t = opp[level], direct[level]

        def go(n, r0, q, dst, dev):
            rs[s, level, n] = send(part.at[where(s, r0, {**fixed, d: q})], dst, rs_s.at[s, level, n],
                                   rs_r.at[s, level, n], dev)

        go(0, 0, far, o.at[s, 0], to_plus)
        go(1, 2, far, o.at[s, 1], to_minus)
        go(2, 2, plus, t.at[s, 0, pl.ds(2, 2)], to_plus)
        go(3, 0, minus, t.at[s, 1, pl.ds(0, 2)], to_minus)

    def rs_forward(s, level):
        d = ORDER[s][level]
        p = coord[d]
        fixed = fixed_of(s, level)
        plus, minus = lax.rem(p + 1, 4), lax.rem(p + 3, 4)
        o, t = opp[level], direct[level]
        for n, r0, q, side in ((4, 0, plus, 0), (5, 2, minus, 1)):
            rs[s, level, side].wait_recv()
            at = where(s, r0, {**fixed, d: q})
            part[at] = (part[at].astype(F32) + o[s, side].astype(F32)).astype(BF)
            rs[s, level, n] = send(part.at[at], t.at[s, side, pl.ds(r0, 2)], rs_s.at[s, level, n],
                                   rs_r.at[s, level, n], at_axis(d, q))

    def rs_finish(s, level):
        for n in (2, 3, 4, 5):
            rs[s, level, n].wait_recv()
        fixed = fixed_of(s, level + 1)
        t = direct[level]
        total = []
        for r0 in (0, 2):
            at = where(s, r0, fixed)
            v = part[at].astype(F32) + t[s, 0, pl.ds(r0, 2)].astype(F32) + t[s, 1, pl.ds(r0, 2)].astype(F32)
            if level < 2:
                part[at] = v.astype(BF)
            else:
                total.append(v.reshape(32, 128))
        return total

    for s in range(3):
        rs_send(s, 0)

    @pl.loop(0, 8)
    def _(k):
        half = lax.div(k, 4)
        lanes = pl.ds(pl.multiple_of(lax.rem(k, 4) * 128, 128), 128)
        col = jnp.transpose(jnp.broadcast_to(idxs[half, 0:1, lanes], (128, 128)))
        rows = pl.ds(pl.multiple_of(k * 128, 128), 128)
        lane = lax.broadcasted_iota(jnp.int32, (128, 128), 1)
        for n in range(NB // 128):
            oht[rows, 128 * n:128 * (n + 1)] = jnp.where(col == lane + 128 * n, 1.0, 0.0).astype(BF)

    sums = {}
    for level in range(3):
        for s in range(3):
            if level:
                rs_finish(s, level - 1)
                rs_send(s, level)
        for s in range(3):
            rs_forward(s, level)
    for s in range(3):
        sums[s] = jnp.concatenate(rs_finish(s, 2), axis=0)

    power = sums[0] * sums[0] + sums[1] * sums[1] + sums[2] * sums[2]
    psum[c] = power
    p_copy = send(psum.at[c], psum.at[c], core_s.at[2], core_r.at[2], partner)
    p_copy.wait_recv()
    power = jnp.sum(psum[0] + psum[1], axis=1, keepdims=True) / NF
    scale = lax.rsqrt(power + 1e-06)
    for s in range(3):
        v = (sums[s] * scale).astype(BF).reshape(4, 16, 128)
        for r0 in (0, 2):
            pilot[where(s, r0, fixed_of(s, 3))] = v[r0:r0 + 2]

    ag = {}

    def ag_send(s, level):
        d = ORDER[s][level]
        p = coord[d]
        fixed = fixed_of(s, level + 1)
        to_plus, to_minus = at_axis(d, lax.rem(p + 1, 4)), at_axis(d, lax.rem(p + 3, 4))
        for n, r0, dev in ((0, 0, to_plus), (1, 2, to_minus), (2, 2, to_plus), (3, 0, to_minus)):
            ref = pilot.at[where(s, r0, fixed)]
            ag[s, level, n] = send(ref, ref, ag_s.at[s, level, n], ag_r.at[s, level, n], dev)

    def ag_forward(s, level):
        d = ORDER[s][level]
        p = coord[d]
        plus, minus = lax.rem(p + 1, 4), lax.rem(p + 3, 4)
        for n, r0, q, dev in ((4, 0, minus, plus), (5, 2, plus, minus)):
            ag[s, level, n - 4].wait_recv()
            ref = pilot.at[where(s, r0, {**fixed_of(s, level), d: q})]
            ag[s, level, n] = send(ref, ref, ag_s.at[s, level, n], ag_r.at[s, level, n], at_axis(d, dev))

    def ag_finish(s, level):
        for n in (2, 3, 4, 5):
            ag[s, level, n].wait_recv()

    for level in (2, 1, 0):
        for s in range(3):
            if level < 2:
                ag_finish(s, level + 1)
            ag_send(s, level)
        for s in range(3):
            ag_forward(s, level)

    shot_row = jnp.concatenate([idxs[0, 1:2, :], idxs[1, 1:2, :]], axis=1)
    shot_mem = jnp.where(lax.broadcasted_iota(jnp.int32, (SHOT_DEV, 2 * TR), 0) == shot_row, 1.0, 0.0).astype(BF)
    rcv_mem = [jnp.where(lax.broadcasted_iota(jnp.int32, (RCV_DEV, TR), 0) == idxs[h, 2:3, :], 1.0, 0.0).astype(BF)
               for h in range(2)]

    @pl.loop(0, 8)
    def _(k):
        half = lax.div(k, 4)
        lanes = pl.ds(pl.multiple_of(lax.rem(k, 4) * 128, 128), 128)
        rows = pl.ds(pl.multiple_of(k * 128, 128), 128)
        lane = lax.broadcasted_iota(jnp.int32, (128, 128), 1)
        col = jnp.transpose(jnp.broadcast_to(idxs[half, 1:2, lanes], (128, 128)))
        shot_one[rows] = jnp.where(col == lane, 1.0, 0.0).astype(BF)
        col = jnp.transpose(jnp.broadcast_to(idxs[half, 2:3, lanes], (128, 128)))
        for n in range(2):
            rcv_one[rows, 128 * n:128 * (n + 1)] = jnp.where(col == lane + 128 * n, 1.0, 0.0).astype(BF)

    for s in range(3):
        ag_finish(s, 0)

    low = low_half(128)

    @pl.loop(0, 8)
    def _(k):
        rows = pl.ds(pl.multiple_of(k * 128, 128), 128)
        inner = pl.ds(pl.multiple_of(lax.rem(k, 4) * 128, 128), 128)
        a = oht[rows]
        for s in range(3):
            lanes = slice(128 * s, 128 * (s + 1))
            row = dot(a, pilot[s].reshape(NB, 128))
            cross[rows, lanes] = times_conj(spec[lax.div(k, 4), inner, lanes].astype(F32), row, low)

    def split(v):
        hi = v.astype(BF)
        return hi, (v - hi.astype(F32)).astype(BF)

    jac = {}

    def reduce_phases(sweep, toward_shot, toward_rcv):
        hi, lo = split(toward_shot)
        zs_st[sweep] = (dot(shot_mem, hi) + dot(shot_mem, lo)).astype(BF)
        for h in range(2):
            hi, lo = split(toward_rcv[TR * h:TR * (h + 1)])
            zr_st[RCV_DEV * h:RCV_DEV * (h + 1)] = (dot(rcv_mem[h], hi) + dot(rcv_mem[h], lo)).astype(BF)
        exchange = []
        for k in range(1, 16):
            to = lax.rem(i + k, 16)
            exchange.append(send(zr_st.at[pl.ds(pl.multiple_of(to * 32, 32), 32)], zr_rv.at[sweep, i],
                                 jr_s.at[2 * sweep, k], jr_r.at[2 * sweep, k], plane[k - 1]))
        for k in range(1, 4):
            to = lax.rem(y + k, 4)
            exchange.append(send(zs_st.at[sweep, pl.ds(pl.multiple_of(to * 32, 32), 32)], zs_rv.at[sweep, y],
                                 js_s.at[2 * sweep, k], js_r.at[2 * sweep, k], line[k - 1]))
        my_shot = pl.ds(pl.multiple_of(y * 32, 32), 32)
        my_rcv = pl.ds(pl.multiple_of(i * 32, 32), 32)
        zr_rv[sweep, i] = zr_st[my_rcv]
        zs_rv[sweep, y] = zs_st[sweep, my_shot]
        for copy in exchange:
            copy.wait()
        zs = zs_rv[sweep, 0].astype(F32)
        for k in range(1, 4):
            zs += zs_rv[sweep, k].astype(F32)
        zr = zr_rv[sweep, 0].astype(F32)
        for k in range(1, 16):
            zr += zr_rv[sweep, k].astype(F32)
        shot_ph[sweep, my_shot] = jnp.concatenate([soften(zs[:, 128 * s:128 * (s + 1)]) for s in range(3)], axis=1).astype(BF)
        rcv_ph[sweep, my_rcv] = jnp.concatenate([soften(zr[:, 128 * s:128 * (s + 1)]) for s in range(3)], axis=1).astype(BF)
        gather = []
        ref = rcv_ph.at[sweep, my_rcv]
        for k in range(1, 16):
            gather.append(send(ref, ref, jr_s.at[2 * sweep + 1, k], jr_r.at[2 * sweep + 1, k], plane[k - 1]))
        ref = shot_ph.at[sweep, my_shot]
        for k in range(1, 4):
            gather.append(send(ref, ref, js_s.at[2 * sweep + 1, k], js_r.at[2 * sweep + 1, k], line[k - 1]))
        for copy in gather:
            copy.wait()

    reduce_phases(0, cross[...], cross[...])

    def turned(one, phases, rows):
        at = dot(one, phases)
        v = cross[rows]
        mask = low_half(v.shape[0])
        return jnp.concatenate([times_conj(v[:, 128 * s:128 * (s + 1)], at[:, 128 * s:128 * (s + 1)], mask)
                                for s in range(3)], axis=1)

    toward_shot = jnp.concatenate([turned(rcv_one[pl.ds(TR * h, TR)], rcv_ph[0, pl.ds(RCV_DEV * h, RCV_DEV)],
                                          pl.ds(TR * h, TR)) for h in range(2)], axis=0)
    toward_rcv = turned(shot_one[...], shot_ph[0], pl.ds(0, 2 * TR))
    reduce_phases(1, toward_shot, toward_rcv)

    theirs = rcv_ph.at[1, pl.ds(pl.multiple_of(oc * RCV_DEV, RCV_DEV), RCV_DEV)]
    last = [send(theirs, rcv_all.at[c], core_s.at[3], core_r.at[3], partner),
            send(shot_ph.at[1], shot_all.at[c], core_s.at[4], core_r.at[4], partner)]
    rcv_all[c] = rcv_ph[1, pl.ds(pl.multiple_of(c * RCV_DEV, RCV_DEV), RCV_DEV)]
    shot_all[c] = shot_ph[1]
    for copy in last:
        copy.wait_recv()
    for src, dst, n in ((shot_all, shot_out, SHOT_DEV), (rcv_all, rcv_out, RCV_DEV)):
        mask = low_half(n)
        groups = [src[h, :, 128 * s:128 * (s + 1)].astype(F32) for h in range(2) for s in range(3)]
        for t in range(3):
            a, b = groups[2 * t], groups[2 * t + 1]
            dst[0, :, 128 * t:128 * (t + 1)] = jnp.where(mask, a, swap(b))
            dst[1, :, 128 * t:128 * (t + 1)] = jnp.where(mask, swap(a), b)

    for copy in [idx_copy, p_copy] + last + list(rs.values()) + list(ag.values()):
        copy.wait_send()


def shards(table, traces, cmp_bin, shot_index, rcv_index, live):
    rows = [
        jnp.where(live != 0, cmp_bin, -1),
        shot_index - lax.axis_index("shot") * SHOT_DEV,
        rcv_index - lax.axis_index("rcv") * RCV_DEV,
    ]
    idx = jnp.stack(rows + [jnp.zeros_like(live)] * 5)
    vmem = pl.BlockSpec(memory_space=pltpu.VMEM)
    dma = pltpu.SemaphoreType.DMA
    return pl.pallas_call(
        kernel,
        out_shape=(
            jax.ShapeDtypeStruct((2, SHOT_DEV, NF), F32),
            jax.ShapeDtypeStruct((2, RCV_DEV, NF), F32),
        ),
        in_specs=[vmem] * 3,
        out_specs=(vmem, vmem),
        scratch_shapes=[
            pltpu.VMEM((2, TR, HC), BF),
            pltpu.VMEM((2, 8, TR), jnp.int32),
            pltpu.VMEM((NB, 2 * TR), BF),
            pltpu.VMEM((2 * TR, NB), BF),
            pltpu.VMEM((3, 4, 4, 4, 4, 16, 128), BF),
            pltpu.VMEM((3, 4, 4, 4, 4, 16, 128), BF),
            pltpu.VMEM((2 * TR, HC), F32),
            pltpu.VMEM((2, 64, 128), F32),
            pltpu.VMEM((2 * TR, SHOT_DEV), BF),
            pltpu.VMEM((2 * TR, RCV_DEV), BF),
            pltpu.VMEM((2, SHOT_DEV, HC), BF),
            pltpu.VMEM((2 * RCV_DEV, HC), BF),
            pltpu.VMEM((2, 4, 32, HC), BF),
            pltpu.VMEM((2, 16, 32, HC), BF),
            pltpu.VMEM((2, SHOT_DEV, HC), BF),
            pltpu.VMEM((2, 2 * RCV_DEV, HC), BF),
            pltpu.VMEM((2, SHOT_DEV, HC), BF),
            pltpu.VMEM((2, RCV_DEV, HC), BF),
            pltpu.VMEM((3, 2, 2, 4, 4, 16, 128), BF),
            pltpu.VMEM((3, 2, 2, 4, 16, 128), BF),
            pltpu.VMEM((3, 2, 2, 16, 128), BF),
            pltpu.VMEM((3, 2, 4, 4, 4, 16, 128), BF),
            pltpu.VMEM((3, 2, 4, 4, 16, 128), BF),
            pltpu.VMEM((3, 2, 4, 16, 128), BF),
            dma((5,)),
            dma((5,)),
            dma((3, 3, 6)),
            dma((3, 3, 6)),
            dma((3, 3, 6)),
            dma((3, 3, 6)),
            dma((4, 4)),
            dma((4, 4)),
            dma((4, 16)),
            dma((4, 16)),
        ],
        compiler_params=pltpu.CompilerParams(
            collective_id=0, has_side_effects=True, vmem_limit_bytes=56 * 1024 * 1024
        ),
    )(traces, table, idx)


def solution(mesh):
    split = P(("shot", "rcv"))
    table = dft_halves()

    def run(traces, cmp_bin, shot_index, rcv_index, live):
        return jax.shard_map(
            shards,
            mesh=mesh,
            in_specs=(P(), P(("shot", "rcv"), None), split, split, split, split),
            out_specs=(P(None, "shot", None), P(None, "rcv", None)),
            check_vma=False,
        )(jnp.asarray(table), traces, cmp_bin, shot_index, rcv_index, live)

    return run
```

```python
import functools
import math

import jax
import jax.numpy as jnp
import numpy as np
from jax import lax
from jax.experimental import pallas as pl
from jax.experimental.pallas import tpu as pltpu
from jax.sharding import PartitionSpec as P

NT = 2000
NF = 384
FLO = 20
SHOT_DEV = 128
RCV_DEV = 256
TR = 512
NB = 4096
HC = NF
MESH = pl.DeviceIdType.MESH
ORDER = ((0, 1, 2), (1, 2, 0), (2, 0, 1))
BF = jnp.bfloat16
F32 = jnp.float32


def dft_halves():
    sample = np.arange(NT, dtype=np.int32)
    band = FLO + np.arange(NF, dtype=np.int32)
    angles = (band[:, None] * sample[None, :] % NT).astype(np.float32) * np.float32(2.0 * math.pi / NT)
    factor = np.float32(1.0 / math.sqrt(NT))
    re, im = np.cos(angles) * factor, -np.sin(angles) * factor
    halves = [np.concatenate([re[a:a + 128], im[a:a + 128], re[b:b + 64], im[b:b + 64]])
              for a, b in ((0, 128), (256, 192))]
    return np.stack(halves).astype(jnp.bfloat16)


def dot(a, b):
    return jnp.dot(a, b, preferred_element_type=F32)


def swap(v):
    return pltpu.roll(v, 64, axis=1)


def low_half(rows):
    return lax.broadcasted_iota(jnp.int32, (rows, 128), 1) < 64


def times_conj(a, b, low):
    same = a[2] * b[2]
    mixed = a[2] * swap(b[2])
    return (a[0] * b[0] + a[1] * b[1], a[1] * b[0] - a[0] * b[1],
            jnp.where(low, same + swap(same), mixed - swap(mixed)))


def soften(v):
    sq = [g * g for g in v]
    scale = lax.rsqrt(sq[0] + sq[1] + 1.0)
    return (v[0] * scale, v[1] * scale, v[2] * lax.rsqrt(sq[2] + swap(sq[2]) + 1.0))


def groups(v):
    return tuple(v[:, 128 * s:128 * (s + 1)] for s in range(3))


def kernel(traces_hbm, table_hbm, cmp_bin, shot_index, rcv_index, live, shot_out, rcv_out,
           traces, table, spec, theirs, idxs, oh, oht, part, pilot, cross, turn, high, rest, psum, member, shot_one, rcv_one,
           zs_st, zr_st, zs_rv, zr_rv, shot_ph, rcv_ph, opp1, dir1, dir2, dir3,
           in_sem, core_s, core_r, rs_s, rs_r, ag_s, ag_r, js_s, js_r, jr_s, jr_r):
    i = lax.axis_index("shot")
    j = lax.axis_index("rcv")
    z, x = lax.div(i, 4), lax.rem(i, 4)
    y, c = lax.div(j, 2), lax.rem(j, 2)
    coord = (x, y, z)
    oc = 1 - c
    partner = (i, 2 * y + oc)

    def at_axis(d, v):
        if d == 0:
            return (z * 4 + v, j)
        if d == 1:
            return (i, 2 * v + c)
        return (v * 4 + x, j)

    plane = [(lax.rem(i + k, 16), j) for k in range(1, 16)]
    line = [at_axis(1, lax.rem(y + k, 4)) for k in range(1, 4)]
    traces_in = pltpu.make_async_copy(traces_hbm, traces, in_sem.at[0])
    table_in = [pltpu.make_async_copy(table_hbm.at[h], table.at[n], in_sem.at[n + 1]) for n, h in enumerate((oc, c))]
    traces_in.start()
    table_in[0].start()
    table_in[1].start()
    barrier = pltpu.get_barrier_semaphore()
    for dev in plane + line + [partner]:
        pl.semaphore_signal(barrier, inc=1, device_id=dev, device_id_type=MESH)

    started = []

    def send(src, dst, s_sem, r_sem, dev):
        copy = pltpu.make_async_remote_copy(src_ref=src, dst_ref=dst, send_sem=s_sem, recv_sem=r_sem, device_id=dev,
                                            device_id_type=MESH)
        copy.start()
        started.append(copy)
        return copy

    idxs[c, 0:1] = jnp.where(live[...] != 0, cmp_bin[...], -1)
    idxs[c, 1:2] = shot_index[...] - i * SHOT_DEV
    idxs[c, 2:3] = rcv_index[...] - j * RCV_DEV
    idxs[c, 3:8] = jnp.zeros((5, TR), jnp.int32)

    def dft(n, dst):
        @pl.loop(0, 3)
        def _(g):
            rows = pl.ds(pl.multiple_of(g * 128, 128), 128)
            v = dot(table[n, rows], traces[...])
            lanes = pl.ds(pl.multiple_of(g * 128, 128), 128)
            dst[:, lanes] = jnp.transpose(v).astype(BF)

    traces_in.wait()
    table_in[0].wait()
    dft(0, theirs)
    pl.semaphore_wait(barrier, 19)
    idx_copy = send(idxs.at[c], idxs.at[c], core_s.at[0], core_r.at[0], partner)
    spec_copy = send(theirs, spec.at[c], core_s.at[1], core_r.at[1], partner)
    table_in[1].wait()
    dft(1, spec.at[c])
    idx_copy.wait_recv()

    bin_row = jnp.concatenate([idxs[0, 0:1, :], idxs[1, 0:1, :]], axis=1)

    @pl.loop(0, NB // 128)
    def _(k):
        bins = lax.broadcasted_iota(jnp.int32, (128, 2 * TR), 0) + k * 128
        oh[pl.ds(pl.multiple_of(k * 128, 128), 128)] = jnp.where(bins == bin_row, 1.0, 0.0).astype(BF)

    spec_copy.wait_recv()

    direct = (None, dir2, dir3)
    rs = {}

    def where(s, r, fixed):
        return (s, r) + tuple(fixed[d] if d in fixed else slice(None) for d in (2, 1, 0))

    def fixed_of(s, level):
        return {d: coord[d] for d in ORDER[s][:level]}

    def slab_send(s, r):
        d = ORDER[s][0]
        near, away = (1, 3) if r % 2 == 0 else (3, 1)
        near, away, far = lax.rem(coord[d] + near, 4), lax.rem(coord[d] + away, 4), lax.rem(coord[d] + 2, 4)
        n = (3 + r, s)
        rs[s, r, 0] = send(part.at[where(s, r, {d: far})], opp1.at[s, r], rs_s.at[n + (0,)], rs_r.at[n + (0,)],
                           at_axis(d, near))
        rs[s, r, 1] = send(part.at[where(s, r, {d: away})], dir1.at[s, r % 2, r], rs_s.at[n + (1,)],
                           rs_r.at[n + (1,)], at_axis(d, away))

    def slab_forward(s, r):
        d = ORDER[s][0]
        near = lax.rem(coord[d] + (1 if r % 2 == 0 else 3), 4)
        rs[s, r, 0].wait_recv()
        at = where(s, r, {d: near})
        part[at] = (part[at].astype(F32) + opp1[s, r].astype(F32)).astype(BF)
        n = (3 + r, s, 2)
        rs[s, r, 2] = send(part.at[at], dir1.at[s, 1 - r % 2, r], rs_s.at[n], rs_r.at[n], at_axis(d, near))

    def slab_finish(s, r):
        rs[s, r, 1].wait_recv()
        rs[s, r, 2].wait_recv()
        at = where(s, r, fixed_of(s, 1))
        part[at] = (part[at].astype(F32) + dir1[s, 0, r].astype(F32) + dir1[s, 1, r].astype(F32)).astype(BF)

    def rs_send(s, level):
        d = ORDER[s][level]
        for k in (2, 1, 3):
            q = lax.rem(coord[d] + k, 4)
            src = part.at[where(s, slice(None), {**fixed_of(s, level), d: q})]
            n = (level, s, k - 1)
            rs[s, level, k, 0] = send(src, direct[level].at[s, k - 1], rs_s.at[n], rs_r.at[n], at_axis(d, q))

    def rs_finish(s, level):
        t = direct[level]
        for k in (1, 2, 3):
            rs[s, level, k, 0].wait_recv()
        at = where(s, slice(None), fixed_of(s, level + 1))
        return (part[at].astype(F32) + t[s, 0].astype(F32)) + (t[s, 1].astype(F32) + t[s, 2].astype(F32))

    for r in range(4):
        v = dot(oh[1024 * r:1024 * (r + 1)], spec[...].reshape(2 * TR, HC)).astype(BF)
        for s in range(3):
            part[s, r] = v[:, 128 * s:128 * (s + 1)].reshape(4, 4, 4, 16, 128)
        for s in range(3):
            slab_send(s, r)

    lane = lax.broadcasted_iota(jnp.int32, (128, 128), 1)

    @pl.loop(0, 8)
    def _(k):
        half = lax.div(k, 4)
        lanes = pl.ds(pl.multiple_of(lax.rem(k, 4) * 128, 128), 128)
        rows = pl.ds(pl.multiple_of(k * 128, 128), 128)
        col = jnp.transpose(jnp.broadcast_to(idxs[half, 0:1, lanes], (128, 128)))
        for n in range(NB // 128):
            oht[rows, 128 * n:128 * (n + 1)] = jnp.where(col == lane + 128 * n, 1.0, 0.0).astype(BF)
        col = jnp.transpose(jnp.broadcast_to(idxs[half, 1:2, lanes], (128, 128)))
        shot_one[rows] = jnp.where(col == lane, 1.0, 0.0).astype(BF)
        col = jnp.transpose(jnp.broadcast_to(idxs[half, 2:3, lanes], (128, 128)))
        for n in range(2):
            rcv_one[rows, 128 * n:128 * (n + 1)] = jnp.where(col == lane + 128 * n, 1.0, 0.0).astype(BF)

    for h in range(2):
        shots = lax.broadcasted_iota(jnp.int32, (SHOT_DEV, TR), 0)
        member[h, :SHOT_DEV] = jnp.where(shots == idxs[h, 1:2, :], 1.0, 0.0).astype(BF)
        rcvs = lax.broadcasted_iota(jnp.int32, (RCV_DEV, TR), 0)
        member[h, SHOT_DEV:] = jnp.where(rcvs == idxs[h, 2:3, :], 1.0, 0.0).astype(BF)

    for r in range(4):
        for s in range(3):
            slab_forward(s, r)
    for s in range(3):
        for r in range(4):
            slab_finish(s, r)
        rs_send(s, 1)
    for s in range(3):
        part[where(s, slice(None), fixed_of(s, 2))] = rs_finish(s, 1).astype(BF)
        rs_send(s, 2)
    sums = [rs_finish(s, 2).reshape(64, 128) for s in range(3)]

    power = sums[0] * sums[0] + sums[1] * sums[1] + sums[2] * sums[2]
    psum[c] = power
    p_copy = send(psum.at[c], psum.at[c], core_s.at[2], core_r.at[2], partner)
    p_copy.wait_recv()
    power = jnp.sum(psum[0] + psum[1], axis=1, keepdims=True) / NF
    scale = lax.rsqrt(power + 1e-06)
    for s in range(3):
        pilot[where(s, slice(None), fixed_of(s, 3))] = (sums[s] * scale).astype(BF).reshape(4, 16, 128)

    ag = {}

    def ag_send(s, level):
        d = ORDER[s][level]
        ref = pilot.at[where(s, slice(None), fixed_of(s, level + 1))]
        for k in (2, 1, 3):
            n = (level, s, k - 1)
            ag[s, level, k] = send(ref, ref, ag_s.at[n], ag_r.at[n], at_axis(d, lax.rem(coord[d] + k, 4)))

    def ag_finish(s, level):
        for k in (1, 2, 3):
            ag[s, level, k].wait_recv()

    def ag_slab(s, r, way):
        d = ORDER[s][0]
        n = (3 + r, s, way)
        ref = pilot.at[where(s, r, fixed_of(s, 1))]
        to = at_axis(d, lax.rem(coord[d] + (1, 3)[way], 4))
        ag[s, r, way, 0] = send(ref, ref, ag_s.at[n], ag_r.at[n], to)

    def ag_forward(s, r):
        d = ORDER[s][0]
        way = r % 2
        ag[s, r, way, 0].wait_recv()
        n = (3 + r, s, 2)
        ref = pilot.at[where(s, r, {d: lax.rem(coord[d] + (3, 1)[way], 4)})]
        ag[s, r, 2, 0] = send(ref, ref, ag_s.at[n], ag_r.at[n], at_axis(d, lax.rem(coord[d] + (1, 3)[way], 4)))

    for s in range(3):
        ag_send(s, 2)
    for s in range(3):
        ag_finish(s, 2)
        ag_send(s, 1)
    for s in range(3):
        ag_finish(s, 1)
        for r in (0, 2):
            ag_slab(s, r, 0)
            ag_slab(s, r + 1, 1)
            ag_slab(s, r, 1)
            ag_slab(s, r + 1, 0)

    for r in range(4):
        for s in range(3):
            ag_forward(s, r)

    for r in range(4):
        for s in range(3):
            ag[s, r, 1 - r % 2, 0].wait_recv()
            ag[s, r, 2, 0].wait_recv()
        v = dot(oht[:, 1024 * r:1024 * (r + 1)],
                jnp.concatenate([pilot[s, r].reshape(1024, 128) for s in range(3)], axis=1))
        if r == 0:
            cross[...] = v
        else:
            cross[...] += v

    low = low_half(128)

    def put_split(rows, v):
        for s in range(3):
            hi = v[s].astype(BF)
            high[rows, 128 * s:128 * (s + 1)] = hi
            rest[rows, 128 * s:128 * (s + 1)] = (v[s] - hi.astype(F32)).astype(BF)

    @pl.loop(0, 8)
    def _(k):
        rows = pl.ds(pl.multiple_of(k * 128, 128), 128)
        inner = pl.ds(pl.multiple_of(lax.rem(k, 4) * 128, 128), 128)
        v = times_conj(groups(spec[lax.div(k, 4), inner].astype(F32)), groups(cross[rows]), low)
        for s in range(3):
            cross[rows, 128 * s:128 * (s + 1)] = v[s]
        put_split(rows, v)

    def soft(v):
        return jnp.concatenate(soften(groups(v)), axis=1).astype(BF)

    my_shot = pl.ds(pl.multiple_of(y * 32, 32), 32)
    my_rcv = pl.ds(pl.multiple_of(i * 32, 32), 32)

    def shots_out(sweep):
        out = []
        for k in (2, 1, 3):
            rows = pl.ds(pl.multiple_of(lax.rem(y + k, 4) * 32, 32), 32)
            out.append(send(zs_st.at[sweep, rows], zs_rv.at[sweep, y], js_s.at[2 * sweep, k], js_r.at[2 * sweep, k],
                            line[k - 1]))
        zs_rv[sweep, y] = zs_st[sweep, my_shot]
        return out

    def rcvs_out(sweep):
        out = []
        for k in (10, 6, 9, 11, 5, 7, 2, 8, 14, 1, 3, 4, 12, 13, 15):
            rows = pl.ds(pl.multiple_of(lax.rem(i + k, 16) * 32, 32), 32)
            out.append(send(zr_st.at[sweep, rows], zr_rv.at[sweep, i], jr_s.at[2 * sweep, k], jr_r.at[2 * sweep, k],
                            plane[k - 1]))
        zr_rv[sweep, i] = zr_st[sweep, my_rcv]
        return out

    def shots_back(sweep, arriving):
        for copy in arriving:
            copy.wait_recv()
        zs = zs_rv[sweep, 0].astype(F32)
        for k in range(1, 4):
            zs += zs_rv[sweep, k].astype(F32)
        shot_ph[sweep, my_shot] = soft(zs)
        ref = shot_ph.at[sweep, my_shot]
        return [send(ref, ref, js_s.at[2 * sweep + 1, k], js_r.at[2 * sweep + 1, k], line[k - 1]) for k in (2, 1, 3)]

    def rcvs_back(sweep, arriving):
        for copy in arriving:
            copy.wait_recv()
        zr = zr_rv[sweep, 0].astype(F32)
        for k in range(1, 16):
            zr += zr_rv[sweep, k].astype(F32)
        rcv_ph[sweep, my_rcv] = soft(zr)
        ref = rcv_ph.at[sweep, my_rcv]
        return [send(ref, ref, jr_s.at[2 * sweep + 1, k], jr_r.at[2 * sweep + 1, k], plane[k - 1])
                for k in (10, 6, 9, 11, 5, 7, 2, 8, 14, 1, 3, 4, 12, 13, 15)]

    def received(copies):
        for copy in copies:
            copy.wait_recv()

    both = []
    for h in range(2):
        rows = slice(TR * h, TR * (h + 1))
        both.append(dot(member[h], high[rows]) + dot(member[h], rest[rows]))
        zr_st[0, RCV_DEV * h:RCV_DEV * (h + 1)] = both[h][SHOT_DEV:].astype(BF)
    zs_st[0] = (both[0][:SHOT_DEV] + both[1][:SHOT_DEV]).astype(BF)
    zs1 = shots_out(0)
    zr1 = rcvs_out(0)
    shots1 = shots_back(0, zs1)
    rcvs1 = rcvs_back(0, zr1)

    def turned():
        @pl.loop(0, 8)
        def _(k):
            rows = pl.ds(pl.multiple_of(k * 128, 128), 128)
            put_split(rows, times_conj(groups(cross[rows]), groups(turn[rows]), low))

    received(shots1)
    turn[...] = dot(shot_one[...], shot_ph[0])
    turned()
    for h in range(2):
        rows = slice(TR * h, TR * (h + 1))
        m = member[h, SHOT_DEV:]
        zr_st[1, RCV_DEV * h:RCV_DEV * (h + 1)] = (dot(m, high[rows]) + dot(m, rest[rows])).astype(BF)
    zr2 = rcvs_out(1)
    received(rcvs1)
    for h in range(2):
        rows = slice(TR * h, TR * (h + 1))
        turn[rows] = dot(rcv_one[rows], rcv_ph[0, RCV_DEV * h:RCV_DEV * (h + 1)])
    turned()
    zs = []
    for h in range(2):
        rows = slice(TR * h, TR * (h + 1))
        m = member[h, :SHOT_DEV]
        zs.append(dot(m, high[rows]) + dot(m, rest[rows]))
    zs_st[1] = (zs[0] + zs[1]).astype(BF)
    zs2 = shots_out(1)
    rcvs2 = rcvs_back(1, zr2)
    shots2 = shots_back(1, zs2)

    received(shots2)
    last = [send(shot_ph.at[1], shot_out.at[c], core_s.at[3], core_r.at[3], partner)]
    shot_out[c] = shot_ph[1]
    received(rcvs2)
    away = rcv_ph.at[1, pl.ds(pl.multiple_of(oc * RCV_DEV, RCV_DEV), RCV_DEV)]
    last.append(send(away, rcv_out.at[c], core_s.at[4], core_r.at[4], partner))
    rcv_out[c] = rcv_ph[1, pl.ds(pl.multiple_of(c * RCV_DEV, RCV_DEV), RCV_DEV)]
    received(last)
    for copy in started:
        copy.wait_send()


def unpack(shots, rcvs, shot_out, rcv_out):
    for src, dst, n in ((shots, shot_out, SHOT_DEV), (rcvs, rcv_out, RCV_DEV)):
        mask = low_half(n)
        first, last = (groups(src[h].astype(F32)) for h in range(2))
        for part in range(2):
            dst[part, :, 0:128] = first[part]
            dst[part, :, 256:384] = last[part]
        dst[0, :, 128:256] = jnp.where(mask, first[2], swap(last[2]))
        dst[1, :, 128:256] = jnp.where(mask, swap(first[2]), last[2])


def shards(table, traces, cmp_bin, shot_index, rcv_index, live):
    vmem = pl.BlockSpec(memory_space=pltpu.VMEM)
    hbm = pl.BlockSpec(memory_space=pl.ANY)
    dma = pltpu.SemaphoreType.DMA
    packed = pl.pallas_call(
        kernel,
        out_shape=(
            jax.ShapeDtypeStruct((2, SHOT_DEV, HC), BF),
            jax.ShapeDtypeStruct((2, RCV_DEV, HC), BF),
        ),
        in_specs=[hbm] * 2 + [vmem] * 4,
        out_specs=(vmem, vmem),
        scratch_shapes=[
            pltpu.VMEM((NT, TR), BF),
            pltpu.VMEM((2, HC, NT), BF),
            pltpu.VMEM((2, TR, HC), BF),
            pltpu.VMEM((TR, HC), BF),
            pltpu.VMEM((2, 8, TR), jnp.int32),
            pltpu.VMEM((NB, 2 * TR), BF),
            pltpu.VMEM((2 * TR, NB), BF),
            pltpu.VMEM((3, 4, 4, 4, 4, 16, 128), BF),
            pltpu.VMEM((3, 4, 4, 4, 4, 16, 128), BF),
            pltpu.VMEM((2 * TR, HC), F32),
            pltpu.VMEM((2 * TR, HC), F32),
            pltpu.VMEM((2 * TR, HC), BF),
            pltpu.VMEM((2 * TR, HC), BF),
            pltpu.VMEM((2, 64, 128), F32),
            pltpu.VMEM((2, SHOT_DEV + RCV_DEV, TR), BF),
            pltpu.VMEM((2 * TR, SHOT_DEV), BF),
            pltpu.VMEM((2 * TR, RCV_DEV), BF),
            pltpu.VMEM((2, SHOT_DEV, HC), BF),
            pltpu.VMEM((2, 2 * RCV_DEV, HC), BF),
            pltpu.VMEM((2, 4, 32, HC), BF),
            pltpu.VMEM((2, 16, 32, HC), BF),
            pltpu.VMEM((2, SHOT_DEV, HC), BF),
            pltpu.VMEM((2, 2 * RCV_DEV, HC), BF),
            pltpu.VMEM((3, 4, 4, 4, 16, 128), BF),
            pltpu.VMEM((3, 2, 4, 4, 4, 16, 128), BF),
            pltpu.VMEM((3, 3, 4, 4, 16, 128), BF),
            pltpu.VMEM((3, 3, 4, 16, 128), BF),
            dma((3,)),
            dma((5,)),
            dma((5,)),
            dma((7, 3, 3)),
            dma((7, 3, 3)),
            dma((7, 3, 3)),
            dma((7, 3, 3)),
            dma((4, 4)),
            dma((4, 4)),
            dma((4, 16)),
            dma((4, 16)),
        ],
        compiler_params=pltpu.CompilerParams(
            collective_id=0, has_side_effects=True, vmem_limit_bytes=56 * 1024 * 1024
        ),
    )(traces.T, table, *(v.reshape(1, TR) for v in (cmp_bin, shot_index, rcv_index, live)))
    return pl.pallas_call(
        unpack,
        out_shape=(
            jax.ShapeDtypeStruct((2, SHOT_DEV, NF), F32),
            jax.ShapeDtypeStruct((2, RCV_DEV, NF), F32),
        ),
        in_specs=[vmem] * 2,
        out_specs=(vmem, vmem),
    )(*packed)


def solution(mesh):
    split = P(("shot", "rcv"))
    table = dft_halves()

    def run(traces, cmp_bin, shot_index, rcv_index, live):
        return jax.shard_map(
            shards,
            mesh=mesh,
            in_specs=(P(), P(("shot", "rcv"), None), split, split, split, split),
            out_specs=(P(None, "shot", None), P(None, "rcv", None)),
            check_vma=False,
        )(jnp.asarray(table), traces, cmp_bin, shot_index, rcv_index, live)

    return run
```

```python
import itertools
import math

import jax
import jax.numpy as jnp
import numpy as np
from jax import lax
from jax.experimental import pallas as pl
from jax.experimental.pallas import tpu as pltpu
from jax.sharding import PartitionSpec as P

NT = 2000
NF = 384
FLO = 20
SHOT_DEV = 128
RCV_DEV = 256
TR = 512
NB = 4096
HC = NF
MESH = pl.DeviceIdType.MESH
ORDER = ((0, 1, 2), (1, 2, 0), (2, 0, 1))
BF = jnp.bfloat16
F32 = jnp.float32


def dft_halves():
    sample = np.arange(NT, dtype=np.int32)
    band = FLO + np.arange(NF, dtype=np.int32)
    angles = (band[:, None] * sample[None, :] % NT).astype(np.float32) * np.float32(2.0 * math.pi / NT)
    factor = np.float32(1.0 / math.sqrt(NT))
    re, im = np.cos(angles) * factor, -np.sin(angles) * factor
    halves = [np.concatenate([re[a:a + 128], im[a:a + 128], re[b:b + 64], im[b:b + 64]])
              for a, b in ((0, 128), (256, 192))]
    return np.stack(halves).astype(jnp.bfloat16)


def dot(a, b):
    return jnp.dot(a, b, preferred_element_type=F32)


def swap(v):
    return pltpu.roll(v, 64, axis=1)


def low_half(rows):
    return lax.broadcasted_iota(jnp.int32, (rows, 128), 1) < 64


def times_conj(a, b, low):
    same = a[2] * b[2]
    mixed = a[2] * swap(b[2])
    return (a[0] * b[0] + a[1] * b[1], a[1] * b[0] - a[0] * b[1],
            jnp.where(low, same + swap(same), mixed - swap(mixed)))


def soften(v):
    sq = [g * g for g in v]
    scale = lax.rsqrt(sq[0] + sq[1] + 1.0)
    return (v[0] * scale, v[1] * scale, v[2] * lax.rsqrt(sq[2] + swap(sq[2]) + 1.0))


def groups(v):
    return tuple(v[:, 128 * s:128 * (s + 1)] for s in range(3))


def kernel(traces_hbm, table_hbm, cmp_bin, shot_index, rcv_index, live, shot_out, rcv_out,
           traces, table, raw, spec, theirs, idxs, oh, oht, part, pilot, cross, turn, high, rest, psum, member, shot_one,
           rcv_one, zs_st, zr_st, zs_rv, zr_rv, shot_ph, rcv_ph, opp1, dir1, dir2, dir3, sems):
    i = lax.axis_index("shot")
    j = lax.axis_index("rcv")
    z, x = lax.div(i, 4), lax.rem(i, 4)
    y, c = lax.div(j, 2), lax.rem(j, 2)
    coord = (x, y, z)
    oc = 1 - c
    partner = (i, 2 * y + oc)
    numbers = itertools.count()

    def new_sem():
        return sems.at[next(numbers)]

    def at_axis(d, v):
        if d == 0:
            return (z * 4 + v, j)
        if d == 1:
            return (i, 2 * v + c)
        return (v * 4 + x, j)

    def fetch(src, dst, sem):
        copy = pltpu.make_async_copy(src, dst, sem)
        copy.start()
        return copy

    raw_sem, traces_sem = new_sem(), new_sem()
    for n, ref in enumerate((cmp_bin, shot_index, rcv_index, live)):
        fetch(ref, raw.at[n], raw_sem)
    for n in range(4):
        rows = pl.ds(512 * n, min(512, NT - 512 * n))
        fetch(traces_hbm.at[rows], traces.at[rows], traces_sem)
    table_in = [[fetch(table_hbm.at[h, pl.ds(128 * g, 128)], table.at[n, pl.ds(128 * g, 128)], new_sem())
                 for g in range(3)] for n, h in enumerate((oc, c))]

    barrier = pltpu.get_barrier_semaphore()
    for d in range(3):
        for k in (2, 1, 3):
            pl.semaphore_signal(barrier, inc=1, device_id=at_axis(d, lax.rem(coord[d] + k, 4)), device_id_type=MESH)
    pl.semaphore_signal(barrier, inc=1, device_id=partner, device_id_type=MESH)

    started = []

    def send(src, dst, s_sem, r_sem, dev):
        copy = pltpu.make_async_remote_copy(src_ref=src, dst_ref=dst, send_sem=s_sem, recv_sem=r_sem, device_id=dev,
                                            device_id_type=MESH)
        copy.start()
        return copy

    def arrived(ref, sem):
        pltpu.make_async_remote_copy(src_ref=ref, dst_ref=ref, send_sem=sem, recv_sem=sem, device_id=partner,
                                     device_id_type=MESH).wait_recv()

    def sent(ref, sem):
        pltpu.make_async_remote_copy(src_ref=ref, dst_ref=ref, send_sem=sem, recv_sem=sem, device_id=partner,
                                     device_id_type=MESH).wait_send()

    pltpu.make_async_copy(raw, raw, raw_sem).wait()
    idxs[c, 0:1] = jnp.where(raw[3] != 0, raw[0], -1)
    idxs[c, 1:2] = raw[1] - i * SHOT_DEV
    idxs[c, 2:3] = raw[2] - j * RCV_DEV
    idxs[c, 3:8] = jnp.zeros((5, TR), jnp.int32)
    pltpu.make_async_copy(traces, traces, traces_sem).wait()

    def dft(n, dst):
        for g in range(3):
            table_in[n][g].wait()
            v = dot(table[n, 128 * g:128 * (g + 1)], traces[...])
            dst[:, 128 * g:128 * (g + 1)] = jnp.transpose(v).astype(BF)

    dft(0, theirs)
    pl.semaphore_wait(barrier, 10)
    idx_copy = send(idxs.at[c], idxs.at[c], new_sem(), new_sem(), partner)
    spec_copy = send(theirs, spec.at[c], new_sem(), new_sem(), partner)
    dft(1, spec.at[c])
    idx_copy.wait()

    bin_row = jnp.concatenate([idxs[0, 0:1, :], idxs[1, 0:1, :]], axis=1)

    @pl.loop(0, NB // 128)
    def _(k):
        bins = lax.broadcasted_iota(jnp.int32, (128, 2 * TR), 0) + k * 128
        oh[pl.ds(pl.multiple_of(k * 128, 128), 128)] = jnp.where(bins == bin_row, 1.0, 0.0).astype(BF)

    spec_copy.wait()

    def where(s, r, fixed):
        return (s, r) + tuple(fixed[d] if d in fixed else slice(None) for d in (2, 1, 0))

    def fixed_of(s, level):
        return {d: coord[d] for d in ORDER[s][:level]}

    def halves():
        return [[new_sem() for _ in range(2)] for _ in range(3)]

    slabs_out, level1_out, level2_out = new_sem(), new_sem(), new_sem()
    far_in = [[new_sem() for _ in range(4)] for _ in range(3)]
    slabs_in, level1_in, level2_in = halves(), halves(), [new_sem() for _ in range(3)]

    def slab_send(s, r):
        d = ORDER[s][0]
        near, away = (1, 3) if r % 2 == 0 else (3, 1)
        near, away, far = lax.rem(coord[d] + near, 4), lax.rem(coord[d] + away, 4), lax.rem(coord[d] + 2, 4)
        send(part.at[where(s, r, {d: far})], opp1.at[s, r], slabs_out, far_in[s][r], at_axis(d, near))
        send(part.at[where(s, r, {d: away})], dir1.at[s, r % 2, r], slabs_out, slabs_in[s][r // 2], at_axis(d, away))

    def slab_forward(s, r):
        d = ORDER[s][0]
        near = lax.rem(coord[d] + (1 if r % 2 == 0 else 3), 4)
        arrived(opp1.at[s, r], far_in[s][r])
        at = where(s, r, {d: near})
        part[at] = (part[at].astype(F32) + opp1[s, r].astype(F32)).astype(BF)
        send(part.at[at], dir1.at[s, 1 - r % 2, r], slabs_out, slabs_in[s][r // 2], at_axis(d, near))

    def slab_finish(s, half):
        arrived(dir1.at[s, :, pl.ds(2 * half, 2)], slabs_in[s][half])
        at = where(s, pl.ds(2 * half, 2), fixed_of(s, 1))
        rows = pl.ds(2 * half, 2)
        part[at] = (part[at].astype(F32) + dir1[s, 0, rows].astype(F32) + dir1[s, 1, rows].astype(F32)).astype(BF)
        d = ORDER[s][1]
        for k in (2, 1, 3):
            q = lax.rem(coord[d] + k, 4)
            src = part.at[where(s, rows, {**fixed_of(s, 1), d: q})]
            send(src, dir2.at[s, k - 1, rows], level1_out, level1_in[s][half], at_axis(d, q))

    def level1_finish(s):
        for half in range(2):
            rows = pl.ds(2 * half, 2)
            arrived(dir2.at[s, :, rows], level1_in[s][half])
            at = where(s, rows, fixed_of(s, 2))
            v = [dir2[s, k, rows].astype(F32) for k in range(3)]
            part[at] = ((part[at].astype(F32) + v[0]) + (v[1] + v[2])).astype(BF)
        d = ORDER[s][2]
        for k in (2, 1, 3):
            q = lax.rem(coord[d] + k, 4)
            src = part.at[where(s, slice(None), {**fixed_of(s, 2), d: q})]
            send(src, dir3.at[s, k - 1], level2_out, level2_in[s], at_axis(d, q))

    def level2_finish(s):
        arrived(dir3.at[s], level2_in[s])
        v = [dir3[s, k].astype(F32) for k in range(3)]
        own = part[where(s, slice(None), fixed_of(s, 3))].astype(F32)
        return ((own + v[0]) + (v[1] + v[2])).reshape(64, 128)

    for r in range(4):
        v = dot(oh[1024 * r:1024 * (r + 1)], spec[...].reshape(2 * TR, HC)).astype(BF)
        for s in range(3):
            part[s, r] = v[:, 128 * s:128 * (s + 1)].reshape(4, 4, 4, 16, 128)
        for s in range(3):
            slab_send(s, r)

    lane = lax.broadcasted_iota(jnp.int32, (128, 128), 1)

    def other_one_hot(lo, hi):
        @pl.loop(lo, hi)
        def _(k):
            half = lax.div(k, 4)
            lanes = pl.ds(pl.multiple_of(lax.rem(k, 4) * 128, 128), 128)
            rows = pl.ds(pl.multiple_of(k * 128, 128), 128)
            col = jnp.transpose(jnp.broadcast_to(idxs[half, 0:1, lanes], (128, 128)))
            for n in range(NB // 128):
                oht[rows, 128 * n:128 * (n + 1)] = jnp.where(col == lane + 128 * n, 1.0, 0.0).astype(BF)
            col = jnp.transpose(jnp.broadcast_to(idxs[half, 1:2, lanes], (128, 128)))
            shot_one[rows] = jnp.where(col == lane, 1.0, 0.0).astype(BF)
            col = jnp.transpose(jnp.broadcast_to(idxs[half, 2:3, lanes], (128, 128)))
            for n in range(2):
                rcv_one[rows, 128 * n:128 * (n + 1)] = jnp.where(col == lane + 128 * n, 1.0, 0.0).astype(BF)

    for h in range(2):
        shots = lax.broadcasted_iota(jnp.int32, (SHOT_DEV, TR), 0)
        member[h, :SHOT_DEV] = jnp.where(shots == idxs[h, 1:2, :], 1.0, 0.0).astype(BF)
        rcvs = lax.broadcasted_iota(jnp.int32, (RCV_DEV, TR), 0)
        member[h, SHOT_DEV:] = jnp.where(rcvs == idxs[h, 2:3, :], 1.0, 0.0).astype(BF)

    for r in range(4):
        for s in range(3):
            slab_forward(s, r)
    other_one_hot(0, 8)
    for half in range(2):
        for s in range(3):
            slab_finish(s, half)
    for s in range(3):
        level1_finish(s)
    sums = [level2_finish(s) for s in range(3)]

    power = sums[0] * sums[0] + sums[1] * sums[1] + sums[2] * sums[2]
    psum[c] = power
    p_copy = send(psum.at[c], psum.at[c], new_sem(), new_sem(), partner)
    p_copy.wait()
    power = jnp.sum(psum[0] + psum[1], axis=1, keepdims=True) / NF
    scale = lax.rsqrt(power + 1e-06)
    for s in range(3):
        pilot[where(s, slice(None), fixed_of(s, 3))] = (sums[s] * scale).astype(BF).reshape(4, 16, 128)

    ag0_out, ag1_out, ag2_out = new_sem(), new_sem(), new_sem()
    ag2_in, ag1_in = [new_sem() for _ in range(3)], halves()
    ag_far = [[new_sem() for _ in range(4)] for _ in range(3)]
    ag_in = [new_sem() for _ in range(4)]

    def ag_slab(s, r, way):
        d = ORDER[s][0]
        ref = pilot.at[where(s, r, fixed_of(s, 1))]
        sem = ag_far[s][r] if way == r % 2 else ag_in[r]
        send(ref, ref, ag0_out, sem, at_axis(d, lax.rem(coord[d] + (1, 3)[way], 4)))

    def ag_forward(s, r):
        d = ORDER[s][0]
        way = r % 2
        ref = pilot.at[where(s, r, {d: lax.rem(coord[d] + (3, 1)[way], 4)})]
        arrived(ref, ag_far[s][r])
        send(ref, ref, ag0_out, ag_in[r], at_axis(d, lax.rem(coord[d] + (1, 3)[way], 4)))

    for s in range(3):
        d = ORDER[s][2]
        ref = pilot.at[where(s, slice(None), fixed_of(s, 3))]
        for k in (2, 1, 3):
            send(ref, ref, ag2_out, ag2_in[s], at_axis(d, lax.rem(coord[d] + k, 4)))
    for s in range(3):
        arrived(dir3.at[s], ag2_in[s])
        d = ORDER[s][1]
        for half in range(2):
            ref = pilot.at[where(s, pl.ds(2 * half, 2), fixed_of(s, 2))]
            for k in (2, 1, 3):
                send(ref, ref, ag1_out, ag1_in[s][half], at_axis(d, lax.rem(coord[d] + k, 4)))
    for half in range(2):
        for s in range(3):
            arrived(dir2.at[s, :, pl.ds(2 * half, 2)], ag1_in[s][half])
            for way in (0, 1):
                ag_slab(s, 2 * half, way)
                ag_slab(s, 2 * half + 1, 1 - way)

    for r in range(4):
        for s in range(3):
            ag_forward(s, r)

    for r in range(4):
        arrived(part.at[:, 0, pl.ds(0, 2)], ag_in[r])
        v = dot(oht[:, 1024 * r:1024 * (r + 1)],
                jnp.concatenate([pilot[s, r].reshape(1024, 128) for s in range(3)], axis=1))
        if r == 0:
            cross[...] = v
        else:
            cross[...] += v

    low = low_half(128)

    def put_split(rows, v):
        for s in range(3):
            hi = v[s].astype(BF)
            high[rows, 128 * s:128 * (s + 1)] = hi
            rest[rows, 128 * s:128 * (s + 1)] = (v[s] - hi.astype(F32)).astype(BF)

    @pl.loop(0, 8)
    def _(k):
        rows = pl.ds(pl.multiple_of(k * 128, 128), 128)
        inner = pl.ds(pl.multiple_of(lax.rem(k, 4) * 128, 128), 128)
        v = times_conj(groups(spec[lax.div(k, 4), inner].astype(F32)), groups(cross[rows]), low)
        for s in range(3):
            cross[rows, 128 * s:128 * (s + 1)] = v[s]
        put_split(rows, v)

    def soft(v):
        return jnp.concatenate(soften(groups(v)), axis=1).astype(BF)

    my_rcv = pl.ds(pl.multiple_of(i * 32, 32), 32)
    shots_sem = [(new_sem(), new_sem()) for _ in range(2)]
    rcvs_sem = [(new_sem(), new_sem()) for _ in range(2)]
    back_sem = [(new_sem(), new_sem()) for _ in range(2)]
    far_first = (10, 6, 9, 11, 5, 7, 2, 8, 14, 1, 3, 4, 12, 13, 15)

    def shots_out(sweep):
        for k in (2, 1, 3):
            send(zs_st.at[sweep], zs_rv.at[sweep, y], *shots_sem[sweep], at_axis(1, lax.rem(y + k, 4)))
        zs_rv[sweep, y] = zs_st[sweep]

    def rcvs_out(sweep):
        for k in far_first:
            to = lax.rem(i + k, 16)
            rows = pl.ds(pl.multiple_of(to * 32, 32), 32)
            send(zr_st.at[sweep, rows], zr_rv.at[sweep, i], *rcvs_sem[sweep], (to, j))
        zr_rv[sweep, i] = zr_st[sweep, my_rcv]

    def shots_in(sweep):
        arrived(zs_rv.at[sweep, pl.ds(0, 3)], shots_sem[sweep][1])
        zs = zs_rv[sweep, 0].astype(F32)
        for k in range(1, 4):
            zs += zs_rv[sweep, k].astype(F32)
        shot_ph[sweep] = soft(zs)

    def rcvs_in(sweep):
        arrived(zr_rv.at[sweep, pl.ds(0, 15)], rcvs_sem[sweep][1])
        zr = zr_rv[sweep, 0].astype(F32)
        for k in range(1, 16):
            zr += zr_rv[sweep, k].astype(F32)
        return soft(zr)

    both = []
    for h in range(2):
        rows = slice(TR * h, TR * (h + 1))
        both.append(dot(member[h], high[rows]) + dot(member[h], rest[rows]))
        zr_st[0, RCV_DEV * h:RCV_DEV * (h + 1)] = both[h][SHOT_DEV:].astype(BF)
    rcvs_out(0)
    zs_st[0] = (both[0][:SHOT_DEV] + both[1][:SHOT_DEV]).astype(BF)
    shots_out(0)
    rcv_ph[0, my_rcv] = rcvs_in(0)
    ref = rcv_ph.at[0, my_rcv]
    for k in far_first:
        send(ref, ref, *back_sem[0], (lax.rem(i + k, 16), j))
    shots_in(0)

    def turned():
        @pl.loop(0, 8)
        def _(k):
            rows = pl.ds(pl.multiple_of(k * 128, 128), 128)
            put_split(rows, times_conj(groups(cross[rows]), groups(turn[rows]), low))

    turn[...] = dot(shot_one[...], shot_ph[0])
    turned()
    for h in range(2):
        rows = slice(TR * h, TR * (h + 1))
        m = member[h, SHOT_DEV:]
        zr_st[1, RCV_DEV * h:RCV_DEV * (h + 1)] = (dot(m, high[rows]) + dot(m, rest[rows])).astype(BF)
    rcvs_out(1)
    arrived(rcv_ph.at[0, pl.ds(0, 480)], back_sem[0][1])
    for h in range(2):
        rows = slice(TR * h, TR * (h + 1))
        turn[rows] = dot(rcv_one[rows], rcv_ph[0, RCV_DEV * h:RCV_DEV * (h + 1)])
    turned()
    zs = []
    for h in range(2):
        rows = slice(TR * h, TR * (h + 1))
        m = member[h, :SHOT_DEV]
        zs.append(dot(m, high[rows]) + dot(m, rest[rows]))
    zs_st[1] = (zs[0] + zs[1]).astype(BF)
    shots_out(1)

    rcv_ph[1, my_rcv] = rcvs_in(1)
    ref = rcv_ph.at[1, my_rcv]
    home = lax.div(i, 8)
    rows = pl.ds(pl.multiple_of(lax.rem(i, 8) * 32, 32), 32)
    for k in far_first:
        send(ref, rcv_out.at[c, rows], *back_sem[1], (lax.rem(i + k, 16), 2 * y + home))

    @pl.when(home == c)
    def _():
        rcv_out[c, rows] = rcv_ph[1, my_rcv]

    @pl.when(home != c)
    def _():
        send(ref, rcv_out.at[c, rows], *back_sem[1], partner)

    shots_in(1)
    last = send(shot_ph.at[1], shot_out.at[c], new_sem(), new_sem(), partner)
    shot_out[c] = shot_ph[1]
    sent(part.at[:, pl.ds(0, 3)], slabs_out)
    sent(dir2, level1_out)
    sent(dir3, level2_out)
    sent(part.at[:, pl.ds(0, 3)], ag0_out)
    sent(dir2, ag1_out)
    sent(dir3, ag2_out)
    for sweep in range(2):
        sent(zs_rv.at[sweep, pl.ds(0, 3)], shots_sem[sweep][0])
        sent(zr_rv.at[sweep, pl.ds(0, 15)], rcvs_sem[sweep][0])
    sent(rcv_ph.at[0, pl.ds(0, 480)], back_sem[0][0])
    last.wait()

    @pl.when(home == c)
    def _():
        sent(rcv_ph.at[1, pl.ds(0, 480)], back_sem[1][0])
        arrived(rcv_ph.at[1, pl.ds(0, 480)], back_sem[1][1])

    @pl.when(home != c)
    def _():
        sent(rcv_ph.at[1], back_sem[1][0])
        arrived(rcv_ph.at[1], back_sem[1][1])


def unpack(shots, rcvs, shot_out, rcv_out):
    for src, dst, n in ((shots, shot_out, SHOT_DEV), (rcvs, rcv_out, RCV_DEV)):
        mask = low_half(n)
        first, last = (groups(src[h].astype(F32)) for h in range(2))
        for part in range(2):
            dst[part, :, 0:128] = first[part]
            dst[part, :, 256:384] = last[part]
        dst[0, :, 128:256] = jnp.where(mask, first[2], swap(last[2]))
        dst[1, :, 128:256] = jnp.where(mask, swap(first[2]), last[2])


def shards(table, traces, cmp_bin, shot_index, rcv_index, live):
    vmem = pl.BlockSpec(memory_space=pltpu.VMEM)
    hbm = pl.BlockSpec(memory_space=pl.ANY)
    dma = pltpu.SemaphoreType.DMA
    packed = pl.pallas_call(
        kernel,
        out_shape=(
            jax.ShapeDtypeStruct((2, SHOT_DEV, HC), BF),
            jax.ShapeDtypeStruct((2, RCV_DEV, HC), BF),
        ),
        in_specs=[hbm] * 6,
        out_specs=(vmem, vmem),
        scratch_shapes=[
            pltpu.VMEM((NT, TR), BF),
            pltpu.VMEM((2, HC, NT), BF),
            pltpu.VMEM((4, 1, TR), jnp.int32),
            pltpu.VMEM((2, TR, HC), BF),
            pltpu.VMEM((TR, HC), BF),
            pltpu.VMEM((2, 8, TR), jnp.int32),
            pltpu.VMEM((NB, 2 * TR), BF),
            pltpu.VMEM((2 * TR, NB), BF),
            pltpu.VMEM((3, 4, 4, 4, 4, 16, 128), BF),
            pltpu.VMEM((3, 4, 4, 4, 4, 16, 128), BF),
            pltpu.VMEM((2 * TR, HC), F32),
            pltpu.VMEM((2 * TR, HC), F32),
            pltpu.VMEM((2 * TR, HC), BF),
            pltpu.VMEM((2 * TR, HC), BF),
            pltpu.VMEM((2, 64, 128), F32),
            pltpu.VMEM((2, SHOT_DEV + RCV_DEV, TR), BF),
            pltpu.VMEM((2 * TR, SHOT_DEV), BF),
            pltpu.VMEM((2 * TR, RCV_DEV), BF),
            pltpu.VMEM((2, SHOT_DEV, HC), BF),
            pltpu.VMEM((2, 2 * RCV_DEV, HC), BF),
            pltpu.VMEM((2, 4, SHOT_DEV, HC), BF),
            pltpu.VMEM((2, 16, 32, HC), BF),
            pltpu.VMEM((2, SHOT_DEV, HC), BF),
            pltpu.VMEM((2, 2 * RCV_DEV, HC), BF),
            pltpu.VMEM((3, 4, 4, 4, 16, 128), BF),
            pltpu.VMEM((3, 2, 4, 4, 4, 16, 128), BF),
            pltpu.VMEM((3, 3, 4, 4, 16, 128), BF),
            pltpu.VMEM((3, 3, 4, 16, 128), BF),
            dma((100,)),
        ],
        compiler_params=pltpu.CompilerParams(
            collective_id=0, has_side_effects=True, vmem_limit_bytes=56 * 1024 * 1024
        ),
    )(traces.T, table, *(v.reshape(1, TR) for v in (cmp_bin, shot_index, rcv_index, live)))
    return pl.pallas_call(
        unpack,
        out_shape=(
            jax.ShapeDtypeStruct((2, SHOT_DEV, NF), F32),
            jax.ShapeDtypeStruct((2, RCV_DEV, NF), F32),
        ),
        in_specs=[vmem] * 2,
        out_specs=(vmem, vmem),
    )(*packed)


def solution(mesh):
    split = P(("shot", "rcv"))
    table = dft_halves()

    def run(traces, cmp_bin, shot_index, rcv_index, live):
        return jax.shard_map(
            shards,
            mesh=mesh,
            in_specs=(P(), P(("shot", "rcv"), None), split, split, split, split),
            out_specs=(P(None, "shot", None), P(None, "rcv", None)),
            check_vma=False,
        )(jnp.asarray(table), traces, cmp_bin, shot_index, rcv_index, live)

    return run
```

```python
import itertools
import math

import jax
import jax.numpy as jnp
import numpy as np
from jax import lax
from jax.experimental import pallas as pl
from jax.experimental.pallas import tpu as pltpu
from jax.sharding import PartitionSpec as P

NT = 2000
NF = 384
FLO = 20
SHOT_DEV = 128
RCV_DEV = 256
TR = 512
NB = 4096
HC = NF
MESH = pl.DeviceIdType.MESH
ORDER = ((0, 1, 2), (1, 2, 0), (2, 0, 1))
FAR_FIRST = ((2, 2), (3, 2), (2, 3), (2, 1), (1, 2), (3, 3), (3, 1), (2, 0), (1, 3), (1, 1), (0, 2), (3, 0), (1, 0), (0, 3), (0, 1))
BF = jnp.bfloat16
F32 = jnp.float32


def dft_halves():
    sample = np.arange(NT, dtype=np.int32)
    band = FLO + np.arange(NF, dtype=np.int32)
    angles = (band[:, None] * sample[None, :] % NT).astype(np.float32) * np.float32(2.0 * math.pi / NT)
    factor = np.float32(1.0 / math.sqrt(NT))
    re, im = np.cos(angles) * factor, -np.sin(angles) * factor
    halves = [np.concatenate([re[a:a + 128], im[a:a + 128], re[b:b + 64], im[b:b + 64]])
              for a, b in ((0, 128), (256, 192))]
    return np.stack(halves).astype(jnp.bfloat16)


def dot(a, b):
    return jnp.dot(a, b, preferred_element_type=F32)


def swap(v):
    return pltpu.roll(v, 64, axis=1)


def low_half(rows):
    return lax.broadcasted_iota(jnp.int32, (rows, 128), 1) < 64


def times_conj(a, b, low):
    same = a[2] * b[2]
    mixed = a[2] * swap(b[2])
    return (a[0] * b[0] + a[1] * b[1], a[1] * b[0] - a[0] * b[1],
            jnp.where(low, same + swap(same), mixed - swap(mixed)))


def soften(v):
    sq = [g * g for g in v]
    scale = lax.rsqrt(sq[0] + sq[1] + 1.0)
    return (v[0] * scale, v[1] * scale, v[2] * lax.rsqrt(sq[2] + swap(sq[2]) + 1.0))


def groups(v):
    return tuple(v[:, 128 * s:128 * (s + 1)] for s in range(3))


def kernel(traces_hbm, table_hbm, cmp_bin, shot_index, rcv_index, live, shot_out, rcv_out,
           traces, table, raw, spec, theirs, idxs, oh, oht, part, pilot, cross, turn, high, rest, power, member, shot_one,
           rcv_one, zs_st, zr_st, zs_rv, zr_rv, shot_ph, rcv_ph, opp1, dir1, dir2, last_in, sems):
    i = lax.axis_index("shot")
    j = lax.axis_index("rcv")
    z, x = lax.div(i, 4), lax.rem(i, 4)
    y, c = lax.div(j, 2), lax.rem(j, 2)
    coord = (x, y, z)
    oc = 1 - c
    partner = (i, 2 * y + oc)
    numbers = itertools.count()

    def new_sem():
        return sems.at[next(numbers)]

    def at_axis(d, v):
        if d == 0:
            return (z * 4 + v, j)
        if d == 1:
            return (i, 2 * v + c)
        return (v * 4 + x, j)

    def fetch(src, dst, sem):
        copy = pltpu.make_async_copy(src, dst, sem)
        copy.start()
        return copy

    raw_sem, traces_sem = new_sem(), new_sem()
    for n, ref in enumerate((cmp_bin, shot_index, rcv_index, live)):
        fetch(ref, raw.at[n], raw_sem)
    for n in range(4):
        rows = pl.ds(512 * n, min(512, NT - 512 * n))
        fetch(traces_hbm.at[rows], traces.at[rows], traces_sem)
    table_in = [[fetch(table_hbm.at[h, pl.ds(128 * g, 128)], table.at[n, pl.ds(128 * g, 128)], new_sem())
                 for g in range(3)] for n, h in enumerate((oc, c))]

    barrier = pltpu.get_barrier_semaphore()
    for d in range(3):
        for k in (2, 1, 3):
            pl.semaphore_signal(barrier, inc=1, device_id=at_axis(d, lax.rem(coord[d] + k, 4)), device_id_type=MESH)
    pl.semaphore_signal(barrier, inc=1, device_id=partner, device_id_type=MESH)

    def send(src, dst, s_sem, r_sem, dev):
        copy = pltpu.make_async_remote_copy(src_ref=src, dst_ref=dst, send_sem=s_sem, recv_sem=r_sem, device_id=dev,
                                            device_id_type=MESH)
        copy.start()
        return copy

    def arrived(ref, sem):
        pltpu.make_async_remote_copy(src_ref=ref, dst_ref=ref, send_sem=sem, recv_sem=sem, device_id=partner,
                                     device_id_type=MESH).wait_recv()

    def sent(ref, sem):
        pltpu.make_async_remote_copy(src_ref=ref, dst_ref=ref, send_sem=sem, recv_sem=sem, device_id=partner,
                                     device_id_type=MESH).wait_send()

    pltpu.make_async_copy(raw, raw, raw_sem).wait()
    idxs[c, 0:1] = jnp.where(raw[3] != 0, raw[0], -1)
    idxs[c, 1:2] = raw[1] - i * SHOT_DEV
    idxs[c, 2:3] = raw[2] - j * RCV_DEV
    idxs[c, 3:8] = jnp.zeros((5, TR), jnp.int32)
    pltpu.make_async_copy(traces, traces, traces_sem).wait()

    def dft(n, dst):
        for g in range(3):
            table_in[n][g].wait()
            v = dot(table[n, 128 * g:128 * (g + 1)], traces[...])
            dst[:, 128 * g:128 * (g + 1)] = jnp.transpose(v).astype(BF)

    dft(0, theirs)
    pl.semaphore_wait(barrier, 10)
    idx_copy = send(idxs.at[c], idxs.at[c], new_sem(), new_sem(), partner)
    spec_copy = send(theirs, spec.at[c], new_sem(), new_sem(), partner)
    dft(1, spec.at[c])
    idx_copy.wait()

    bin_row = jnp.concatenate([idxs[0, 0:1, :], idxs[1, 0:1, :]], axis=1)

    @pl.loop(0, NB // 128)
    def _(k):
        bins = lax.broadcasted_iota(jnp.int32, (128, 2 * TR), 0) + k * 128
        oh[pl.ds(pl.multiple_of(k * 128, 128), 128)] = jnp.where(bins == bin_row, 1.0, 0.0).astype(BF)

    spec_copy.wait()

    def where(s, r, fixed):
        return (s, r) + tuple(fixed[d] if d in fixed else slice(None) for d in (2, 1, 0))

    def fixed_of(s, level):
        return {d: coord[d] for d in ORDER[s][:level]}

    def halves():
        return [[new_sem() for _ in range(2)] for _ in range(3)]

    slabs_out, level1_out, last_out = new_sem(), new_sem(), new_sem()
    far_in = [[new_sem() for _ in range(4)] for _ in range(3)]
    slabs_in, level1_in, last_sem = halves(), halves(), halves()

    def slab_send(s, r):
        d = ORDER[s][0]
        near, away = (1, 3) if r % 2 == 0 else (3, 1)
        near, away, far = lax.rem(coord[d] + near, 4), lax.rem(coord[d] + away, 4), lax.rem(coord[d] + 2, 4)
        send(part.at[where(s, r, {d: far})], opp1.at[s, r], slabs_out, far_in[s][r], at_axis(d, near))
        send(part.at[where(s, r, {d: away})], dir1.at[s, r % 2, r], slabs_out, slabs_in[s][r // 2], at_axis(d, away))

    def slab_forward(s, r):
        d = ORDER[s][0]
        near = lax.rem(coord[d] + (1 if r % 2 == 0 else 3), 4)
        arrived(opp1.at[s, r], far_in[s][r])
        at = where(s, r, {d: near})
        part[at] = (part[at].astype(F32) + opp1[s, r].astype(F32)).astype(BF)
        send(part.at[at], dir1.at[s, 1 - r % 2, r], slabs_out, slabs_in[s][r // 2], at_axis(d, near))

    def slab_finish(s, half):
        arrived(dir1.at[s, :, pl.ds(2 * half, 2)], slabs_in[s][half])
        at = where(s, pl.ds(2 * half, 2), fixed_of(s, 1))
        rows = pl.ds(2 * half, 2)
        part[at] = (part[at].astype(F32) + dir1[s, 0, rows].astype(F32) + dir1[s, 1, rows].astype(F32)).astype(BF)
        d = ORDER[s][1]
        for k in (2, 1, 3):
            q = lax.rem(coord[d] + k, 4)
            src = part.at[where(s, rows, {**fixed_of(s, 1), d: q})]
            send(src, dir2.at[s, k - 1, rows], level1_out, level1_in[s][half], at_axis(d, q))

    def level1_finish(s, half):
        rows = pl.ds(2 * half, 2)
        arrived(dir2.at[s, :, rows], level1_in[s][half])
        at = where(s, rows, fixed_of(s, 2))
        v = [dir2[s, k, rows].astype(F32) for k in range(3)]
        v = ((part[at].astype(F32) + v[0]) + (v[1] + v[2])).astype(BF)
        d = ORDER[s][2]
        last_in[s, coord[d], rows] = v
        for k in (2, 1, 3):
            ref = last_in.at[s, coord[d], rows]
            send(ref, ref, last_out, last_sem[s][half], at_axis(d, lax.rem(coord[d] + k, 4)))

    def last_finish(s, half):
        rows = pl.ds(2 * half, 2)
        arrived(last_in.at[s, pl.ds(0, 3), rows], last_sem[s][half])
        v = [last_in[s, k, rows].astype(F32) for k in range(4)]
        pilot[where(s, rows, fixed_of(s, 2))] = ((v[0] + v[1]) + (v[2] + v[3])).astype(BF)

    for r in range(4):
        v = dot(oh[1024 * r:1024 * (r + 1)], spec[...].reshape(2 * TR, HC)).astype(BF)
        for s in range(3):
            part[s, r] = v[:, 128 * s:128 * (s + 1)].reshape(4, 4, 4, 16, 128)
        for s in range(3):
            slab_send(s, r)

    lane = lax.broadcasted_iota(jnp.int32, (128, 128), 1)

    def other_one_hot(lo, hi):
        @pl.loop(lo, hi)
        def _(k):
            half = lax.div(k, 4)
            lanes = pl.ds(pl.multiple_of(lax.rem(k, 4) * 128, 128), 128)
            rows = pl.ds(pl.multiple_of(k * 128, 128), 128)
            col = jnp.transpose(jnp.broadcast_to(idxs[half, 0:1, lanes], (128, 128)))
            for n in range(NB // 128):
                oht[rows, 128 * n:128 * (n + 1)] = jnp.where(col == lane + 128 * n, 1.0, 0.0).astype(BF)
            col = jnp.transpose(jnp.broadcast_to(idxs[half, 1:2, lanes], (128, 128)))
            shot_one[rows] = jnp.where(col == lane, 1.0, 0.0).astype(BF)
            col = jnp.transpose(jnp.broadcast_to(idxs[half, 2:3, lanes], (128, 128)))
            for n in range(2):
                rcv_one[rows, 128 * n:128 * (n + 1)] = jnp.where(col == lane + 128 * n, 1.0, 0.0).astype(BF)

    for h in range(2):
        shots = lax.broadcasted_iota(jnp.int32, (SHOT_DEV, TR), 0)
        member[h, :SHOT_DEV] = jnp.where(shots == idxs[h, 1:2, :], 1.0, 0.0).astype(BF)
        rcvs = lax.broadcasted_iota(jnp.int32, (RCV_DEV, TR), 0)
        member[h, SHOT_DEV:] = jnp.where(rcvs == idxs[h, 2:3, :], 1.0, 0.0).astype(BF)

    for r in range(4):
        for s in range(3):
            slab_forward(s, r)
    other_one_hot(0, 8)
    for half in range(2):
        for s in range(3):
            slab_finish(s, half)
    for half in range(2):
        for s in range(3):
            level1_finish(s, half)

    ag0_out, ag1_out = new_sem(), new_sem()
    ag1_in = halves()
    ag_far = [[new_sem() for _ in range(4)] for _ in range(3)]
    ag_in = [new_sem() for _ in range(4)]

    def ag_slab(s, r, way):
        d = ORDER[s][0]
        ref = pilot.at[where(s, r, fixed_of(s, 1))]
        sem = ag_far[s][r] if way == r % 2 else ag_in[r]
        send(ref, ref, ag0_out, sem, at_axis(d, lax.rem(coord[d] + (1, 3)[way], 4)))

    def ag_forward(s, r):
        d = ORDER[s][0]
        way = r % 2
        ref = pilot.at[where(s, r, {d: lax.rem(coord[d] + (3, 1)[way], 4)})]
        arrived(ref, ag_far[s][r])
        send(ref, ref, ag0_out, ag_in[r], at_axis(d, lax.rem(coord[d] + (1, 3)[way], 4)))

    for half in range(2):
        for s in range(3):
            last_finish(s, half)
            d = ORDER[s][1]
            ref = pilot.at[where(s, pl.ds(2 * half, 2), fixed_of(s, 2))]
            for k in (2, 1, 3):
                send(ref, ref, ag1_out, ag1_in[s][half], at_axis(d, lax.rem(coord[d] + k, 4)))
    for half in range(2):
        for s in range(3):
            arrived(dir2.at[s, :, pl.ds(2 * half, 2)], ag1_in[s][half])
            for way in (0, 1):
                ag_slab(s, 2 * half, way)
                ag_slab(s, 2 * half + 1, 1 - way)

    for r in range(4):
        for s in range(3):
            ag_forward(s, r)

    for r in range(4):
        arrived(part.at[:, 0, pl.ds(0, 2)], ag_in[r])
        v = dot(oht[:, 1024 * r:1024 * (r + 1)],
                jnp.concatenate([pilot[s, r].reshape(1024, 128) for s in range(3)], axis=1))
        if r == 0:
            cross[...] = v
        else:
            cross[...] += v

    low = low_half(128)

    @pl.loop(0, 8)
    def _(k):
        v = groups(cross[pl.ds(pl.multiple_of(k * 128, 128), 128)])
        p = jnp.sum(v[0] * v[0] + v[1] * v[1] + v[2] * v[2], axis=1, keepdims=True)
        power[c, pl.ds(k, 1)] = jnp.transpose(jnp.broadcast_to(p, (128, 128)))[0:1]

    p_copy = send(power.at[c], power.at[c], new_sem(), new_sem(), partner)

    @pl.loop(0, 8)
    def _(k):
        rows = pl.ds(pl.multiple_of(k * 128, 128), 128)
        inner = pl.ds(pl.multiple_of(lax.rem(k, 4) * 128, 128), 128)
        v = times_conj(groups(spec[lax.div(k, 4), inner].astype(F32)), groups(cross[rows]), low)
        for s in range(3):
            cross[rows, 128 * s:128 * (s + 1)] = v[s]

    def put_split(rows, v):
        for s in range(3):
            hi = v[s].astype(BF)
            high[rows, 128 * s:128 * (s + 1)] = hi
            rest[rows, 128 * s:128 * (s + 1)] = (v[s] - hi.astype(F32)).astype(BF)

    p_copy.wait()

    @pl.loop(0, 8)
    def _(k):
        rows = pl.ds(pl.multiple_of(k * 128, 128), 128)
        p = power[0, pl.ds(k, 1)] + power[1, pl.ds(k, 1)]
        scale = lax.rsqrt(jnp.transpose(jnp.broadcast_to(p, (128, 128))) / NF + 1e-06)
        v = [g * scale for g in groups(cross[rows])]
        for s in range(3):
            cross[rows, 128 * s:128 * (s + 1)] = v[s]
        put_split(rows, v)

    def soft(v):
        return jnp.concatenate(soften(groups(v)), axis=1).astype(BF)

    my_rcv = pl.ds(pl.multiple_of(i * 32, 32), 32)
    shots_sem = [(new_sem(), new_sem()) for _ in range(2)]
    rcvs_sem = [(new_sem(), new_sem()) for _ in range(2)]
    back_sem = [(new_sem(), new_sem()) for _ in range(2)]
    plane = [4 * lax.rem(z + kz, 4) + lax.rem(x + kx, 4) for kx, kz in FAR_FIRST]

    def shots_out(sweep):
        for k in (2, 1, 3):
            send(zs_st.at[sweep], zs_rv.at[sweep, y], *shots_sem[sweep], at_axis(1, lax.rem(y + k, 4)))
        zs_rv[sweep, y] = zs_st[sweep]

    def rcvs_out(sweep):
        for to in plane:
            rows = pl.ds(pl.multiple_of(to * 32, 32), 32)
            send(zr_st.at[sweep, rows], zr_rv.at[sweep, i], *rcvs_sem[sweep], (to, j))
        zr_rv[sweep, i] = zr_st[sweep, my_rcv]

    def shots_in(sweep):
        arrived(zs_rv.at[sweep, pl.ds(0, 3)], shots_sem[sweep][1])
        zs = zs_rv[sweep, 0].astype(F32)
        for k in range(1, 4):
            zs += zs_rv[sweep, k].astype(F32)
        shot_ph[sweep] = soft(zs)

    def rcvs_in(sweep):
        arrived(zr_rv.at[sweep, pl.ds(0, 15)], rcvs_sem[sweep][1])
        zr = zr_rv[sweep, 0].astype(F32)
        for k in range(1, 16):
            zr += zr_rv[sweep, k].astype(F32)
        return soft(zr)

    both = []
    for h in range(2):
        rows = slice(TR * h, TR * (h + 1))
        both.append(dot(member[h], high[rows]) + dot(member[h], rest[rows]))
        zr_st[0, RCV_DEV * h:RCV_DEV * (h + 1)] = both[h][SHOT_DEV:].astype(BF)
    zs_st[0] = (both[0][:SHOT_DEV] + both[1][:SHOT_DEV]).astype(BF)
    shots_out(0)
    rcvs_out(0)
    rcv_ph[0, my_rcv] = rcvs_in(0)
    ref = rcv_ph.at[0, my_rcv]
    for to in plane:
        send(ref, ref, *back_sem[0], (to, j))
    shots_in(0)

    def turned():
        @pl.loop(0, 8)
        def _(k):
            rows = pl.ds(pl.multiple_of(k * 128, 128), 128)
            put_split(rows, times_conj(groups(cross[rows]), groups(turn[rows]), low))

    turn[...] = dot(shot_one[...], shot_ph[0])
    turned()
    for h in range(2):
        rows = slice(TR * h, TR * (h + 1))
        m = member[h, SHOT_DEV:]
        zr_st[1, RCV_DEV * h:RCV_DEV * (h + 1)] = (dot(m, high[rows]) + dot(m, rest[rows])).astype(BF)
    rcvs_out(1)
    arrived(rcv_ph.at[0, pl.ds(0, 480)], back_sem[0][1])
    for h in range(2):
        rows = slice(TR * h, TR * (h + 1))
        turn[rows] = dot(rcv_one[rows], rcv_ph[0, RCV_DEV * h:RCV_DEV * (h + 1)])
    turned()
    zs = []
    for h in range(2):
        rows = slice(TR * h, TR * (h + 1))
        m = member[h, :SHOT_DEV]
        zs.append(dot(m, high[rows]) + dot(m, rest[rows]))
    zs_st[1] = (zs[0] + zs[1]).astype(BF)
    shots_out(1)

    rcv_ph[1, my_rcv] = rcvs_in(1)
    ref = rcv_ph.at[1, my_rcv]
    home = lax.div(i, 8)
    rows = pl.ds(pl.multiple_of(lax.rem(i, 8) * 32, 32), 32)
    for to in plane:
        send(ref, rcv_out.at[c, rows], *back_sem[1], (to, 2 * y + home))

    @pl.when(home == c)
    def _():
        rcv_out[c, rows] = rcv_ph[1, my_rcv]

    @pl.when(home != c)
    def _():
        send(ref, rcv_out.at[c, rows], *back_sem[1], partner)

    shots_in(1)
    last = send(shot_ph.at[1], shot_out.at[c], new_sem(), new_sem(), partner)
    shot_out[c] = shot_ph[1]
    sent(part.at[:, pl.ds(0, 3)], slabs_out)
    sent(dir2, level1_out)
    sent(last_in.at[:, pl.ds(0, 3)], last_out)
    sent(part.at[:, pl.ds(0, 3)], ag0_out)
    sent(dir2, ag1_out)
    for sweep in range(2):
        sent(zs_rv.at[sweep, pl.ds(0, 3)], shots_sem[sweep][0])
        sent(zr_rv.at[sweep, pl.ds(0, 15)], rcvs_sem[sweep][0])
    sent(rcv_ph.at[0, pl.ds(0, 480)], back_sem[0][0])
    last.wait()

    @pl.when(home == c)
    def _():
        sent(rcv_ph.at[1, pl.ds(0, 480)], back_sem[1][0])
        arrived(rcv_ph.at[1, pl.ds(0, 480)], back_sem[1][1])

    @pl.when(home != c)
    def _():
        sent(rcv_ph.at[1], back_sem[1][0])
        arrived(rcv_ph.at[1], back_sem[1][1])


def unpack(shots, rcvs, shot_out, rcv_out):
    for src, dst, n in ((shots, shot_out, SHOT_DEV), (rcvs, rcv_out, RCV_DEV)):
        mask = low_half(n)
        first, last = (groups(src[h].astype(F32)) for h in range(2))
        for part in range(2):
            dst[part, :, 0:128] = first[part]
            dst[part, :, 256:384] = last[part]
        dst[0, :, 128:256] = jnp.where(mask, first[2], swap(last[2]))
        dst[1, :, 128:256] = jnp.where(mask, swap(first[2]), last[2])


def shards(table, traces, cmp_bin, shot_index, rcv_index, live):
    vmem = pl.BlockSpec(memory_space=pltpu.VMEM)
    hbm = pl.BlockSpec(memory_space=pl.ANY)
    dma = pltpu.SemaphoreType.DMA
    packed = pl.pallas_call(
        kernel,
        out_shape=(
            jax.ShapeDtypeStruct((2, SHOT_DEV, HC), BF),
            jax.ShapeDtypeStruct((2, RCV_DEV, HC), BF),
        ),
        in_specs=[hbm] * 6,
        out_specs=(vmem, vmem),
        scratch_shapes=[
            pltpu.VMEM((NT, TR), BF),
            pltpu.VMEM((2, HC, NT), BF),
            pltpu.VMEM((4, 1, TR), jnp.int32),
            pltpu.VMEM((2, TR, HC), BF),
            pltpu.VMEM((TR, HC), BF),
            pltpu.VMEM((2, 8, TR), jnp.int32),
            pltpu.VMEM((NB, 2 * TR), BF),
            pltpu.VMEM((2 * TR, NB), BF),
            pltpu.VMEM((3, 4, 4, 4, 4, 16, 128), BF),
            pltpu.VMEM((3, 4, 4, 4, 4, 16, 128), BF),
            pltpu.VMEM((2 * TR, HC), F32),
            pltpu.VMEM((2 * TR, HC), F32),
            pltpu.VMEM((2 * TR, HC), BF),
            pltpu.VMEM((2 * TR, HC), BF),
            pltpu.VMEM((2, 8, 128), F32),
            pltpu.VMEM((2, SHOT_DEV + RCV_DEV, TR), BF),
            pltpu.VMEM((2 * TR, SHOT_DEV), BF),
            pltpu.VMEM((2 * TR, RCV_DEV), BF),
            pltpu.VMEM((2, SHOT_DEV, HC), BF),
            pltpu.VMEM((2, 2 * RCV_DEV, HC), BF),
            pltpu.VMEM((2, 4, SHOT_DEV, HC), BF),
            pltpu.VMEM((2, 16, 32, HC), BF),
            pltpu.VMEM((2, SHOT_DEV, HC), BF),
            pltpu.VMEM((2, 2 * RCV_DEV, HC), BF),
            pltpu.VMEM((3, 4, 4, 4, 16, 128), BF),
            pltpu.VMEM((3, 2, 4, 4, 4, 16, 128), BF),
            pltpu.VMEM((3, 3, 4, 4, 16, 128), BF),
            pltpu.VMEM((3, 4, 4, 4, 16, 128), BF),
            dma((100,)),
        ],
        compiler_params=pltpu.CompilerParams(
            collective_id=0, has_side_effects=True, vmem_limit_bytes=56 * 1024 * 1024
        ),
    )(traces.T, table, *(v.reshape(1, TR) for v in (cmp_bin, shot_index, rcv_index, live)))
    return pl.pallas_call(
        unpack,
        out_shape=(
            jax.ShapeDtypeStruct((2, SHOT_DEV, NF), F32),
            jax.ShapeDtypeStruct((2, RCV_DEV, NF), F32),
        ),
        in_specs=[vmem] * 2,
        out_specs=(vmem, vmem),
    )(*packed)


def solution(mesh):
    split = P(("shot", "rcv"))
    table = dft_halves()

    def run(traces, cmp_bin, shot_index, rcv_index, live):
        return jax.shard_map(
            shards,
            mesh=mesh,
            in_specs=(P(), P(("shot", "rcv"), None), split, split, split, split),
            out_specs=(P(None, "shot", None), P(None, "rcv", None)),
            check_vma=False,
        )(jnp.asarray(table), traces, cmp_bin, shot_index, rcv_index, live)

    return run
```

```python
import itertools
import math

import jax
import jax.numpy as jnp
import numpy as np
from jax import lax
from jax.experimental import pallas as pl
from jax.experimental.pallas import tpu as pltpu
from jax.sharding import PartitionSpec as P

NT = 2000
NF = 384
FLO = 20
SHOT_DEV = 128
RCV_DEV = 256
TR = 512
NB = 4096
HC = NF
MESH = pl.DeviceIdType.MESH
ORDER = ((0, 1, 2), (1, 2, 0), (2, 0, 1))
FAR_FIRST = ((2, 2), (3, 2), (2, 3), (2, 1), (1, 2), (3, 3), (3, 1), (2, 0), (1, 3), (1, 1), (0, 2), (3, 0), (1, 0), (0, 3), (0, 1))
BF = jnp.bfloat16
F32 = jnp.float32


def dft_halves():
    sample = np.arange(NT, dtype=np.int32)
    band = FLO + np.arange(NF, dtype=np.int32)
    angles = (band[:, None] * sample[None, :] % NT).astype(np.float32) * np.float32(2.0 * math.pi / NT)
    factor = np.float32(1.0 / math.sqrt(NT))
    re, im = np.cos(angles) * factor, -np.sin(angles) * factor
    halves = [np.concatenate([re[a:a + 128], im[a:a + 128], re[b:b + 64], im[b:b + 64]])
              for a, b in ((0, 128), (256, 192))]
    return np.stack(halves).astype(jnp.bfloat16)


def dot(a, b):
    return jnp.dot(a, b, preferred_element_type=F32)


def swap(v):
    return pltpu.roll(v, 64, axis=1)


def low_half(rows):
    return lax.broadcasted_iota(jnp.int32, (rows, 128), 1) < 64


def times_conj(a, b, low):
    same = a[2] * b[2]
    mixed = a[2] * swap(b[2])
    return (a[0] * b[0] + a[1] * b[1], a[1] * b[0] - a[0] * b[1],
            jnp.where(low, same + swap(same), mixed - swap(mixed)))


def soften(v):
    sq = [g * g for g in v]
    scale = lax.rsqrt(sq[0] + sq[1] + 1.0)
    return (v[0] * scale, v[1] * scale, v[2] * lax.rsqrt(sq[2] + swap(sq[2]) + 1.0))


def groups(v):
    return tuple(v[:, 128 * s:128 * (s + 1)] for s in range(3))


def kernel(traces_hbm, table_hbm, cmp_bin, shot_index, rcv_index, live, shot_out, rcv_out,
           traces, table, raw, spec, theirs, idxs, oh, oht, part, pilot, cross, turn, high, rest, power, member, shot_one,
           rcv_one, zs_st, zr_st, zs_rv, zr_rv, shot_ph, rcv_ph, opp1, dir1, dir2, last_in, sems):
    i = lax.axis_index("shot")
    j = lax.axis_index("rcv")
    z, x = lax.div(i, 4), lax.rem(i, 4)
    y, c = lax.div(j, 2), lax.rem(j, 2)
    coord = (x, y, z)
    oc = 1 - c
    partner = (i, 2 * y + oc)
    numbers = itertools.count()

    def new_sem():
        return sems.at[next(numbers)]

    def at_axis(d, v):
        if d == 0:
            return (z * 4 + v, j)
        if d == 1:
            return (i, 2 * v + c)
        return (v * 4 + x, j)

    def fetch(src, dst, sem):
        copy = pltpu.make_async_copy(src, dst, sem)
        copy.start()
        return copy

    raw_sem, traces_sem = new_sem(), new_sem()
    for n, ref in enumerate((cmp_bin, shot_index, rcv_index, live)):
        fetch(ref, raw.at[n], raw_sem)
    for n in range(4):
        rows = pl.ds(512 * n, min(512, NT - 512 * n))
        fetch(traces_hbm.at[rows], traces.at[rows], traces_sem)
    table_in = [[fetch(table_hbm.at[h, pl.ds(128 * g, 128)], table.at[n, pl.ds(128 * g, 128)], new_sem())
                 for g in range(3)] for n, h in enumerate((oc, c))]

    barrier = pltpu.get_barrier_semaphore()
    for d in range(3):
        for k in (2, 1, 3):
            pl.semaphore_signal(barrier, inc=1, device_id=at_axis(d, lax.rem(coord[d] + k, 4)), device_id_type=MESH)
    pl.semaphore_signal(barrier, inc=1, device_id=partner, device_id_type=MESH)

    def send(src, dst, s_sem, r_sem, dev):
        copy = pltpu.make_async_remote_copy(src_ref=src, dst_ref=dst, send_sem=s_sem, recv_sem=r_sem, device_id=dev,
                                            device_id_type=MESH)
        copy.start()
        return copy

    def arrived(ref, sem):
        pltpu.make_async_remote_copy(src_ref=ref, dst_ref=ref, send_sem=sem, recv_sem=sem, device_id=partner,
                                     device_id_type=MESH).wait_recv()

    def sent(ref, sem):
        pltpu.make_async_remote_copy(src_ref=ref, dst_ref=ref, send_sem=sem, recv_sem=sem, device_id=partner,
                                     device_id_type=MESH).wait_send()

    pltpu.make_async_copy(raw, raw, raw_sem).wait()
    idxs[c, 0:1] = jnp.where(raw[3] != 0, raw[0], -1)
    idxs[c, 1:2] = raw[1] - i * SHOT_DEV
    idxs[c, 2:3] = raw[2] - j * RCV_DEV
    idxs[c, 3:8] = jnp.zeros((5, TR), jnp.int32)
    pltpu.make_async_copy(traces, traces, traces_sem).wait()

    def dft(n, dst):
        for g in range(3):
            table_in[n][g].wait()
            v = dot(table[n, 128 * g:128 * (g + 1)], traces[...])
            dst[:, 128 * g:128 * (g + 1)] = jnp.transpose(v).astype(BF)

    dft(0, theirs)
    pl.semaphore_wait(barrier, 10)
    idx_copy = send(idxs.at[c], idxs.at[c], new_sem(), new_sem(), partner)
    spec_copy = send(theirs, spec.at[c], new_sem(), new_sem(), partner)
    dft(1, spec.at[c])
    idx_copy.wait()

    bin_row = jnp.concatenate([idxs[0, 0:1, :], idxs[1, 0:1, :]], axis=1)

    @pl.loop(0, NB // 128)
    def _(k):
        bins = lax.broadcasted_iota(jnp.int32, (128, 2 * TR), 0) + k * 128
        oh[pl.ds(pl.multiple_of(k * 128, 128), 128)] = jnp.where(bins == bin_row, 1.0, 0.0).astype(BF)

    spec_copy.wait()

    def where(s, r, fixed):
        return (s, r) + tuple(fixed[d] if d in fixed else slice(None) for d in (2, 1, 0))

    def fixed_of(s, level):
        return {d: coord[d] for d in ORDER[s][:level]}

    def by_slab():
        return [[new_sem() for _ in range(4)] for _ in range(3)]

    slabs_out, level1_out, last_out = new_sem(), new_sem(), new_sem()
    far_in = [[new_sem() for _ in range(4)] for _ in range(3)]
    slabs_in, level1_in, last_sem = by_slab(), by_slab(), by_slab()

    def slab_send(s, r):
        d = ORDER[s][0]
        near, away = (1, 3) if r % 2 == 0 else (3, 1)
        near, away, far = lax.rem(coord[d] + near, 4), lax.rem(coord[d] + away, 4), lax.rem(coord[d] + 2, 4)
        send(part.at[where(s, r, {d: far})], opp1.at[s, r], slabs_out, far_in[s][r], at_axis(d, near))
        send(part.at[where(s, r, {d: away})], dir1.at[s, r % 2, r], slabs_out, slabs_in[s][r], at_axis(d, away))

    def slab_forward(s, r):
        d = ORDER[s][0]
        near = lax.rem(coord[d] + (1 if r % 2 == 0 else 3), 4)
        arrived(opp1.at[s, r], far_in[s][r])
        at = where(s, r, {d: near})
        part[at] = (part[at].astype(F32) + opp1[s, r].astype(F32)).astype(BF)
        send(part.at[at], dir1.at[s, 1 - r % 2, r], slabs_out, slabs_in[s][r], at_axis(d, near))

    def slab_finish(s, r):
        arrived(dir1.at[s, :, pl.ds(r, 1)], slabs_in[s][r])
        at = where(s, pl.ds(r, 1), fixed_of(s, 1))
        rows = pl.ds(r, 1)
        part[at] = (part[at].astype(F32) + dir1[s, 0, rows].astype(F32) + dir1[s, 1, rows].astype(F32)).astype(BF)
        d = ORDER[s][1]
        for k in (2, 1, 3):
            q = lax.rem(coord[d] + k, 4)
            src = part.at[where(s, rows, {**fixed_of(s, 1), d: q})]
            send(src, dir2.at[s, k - 1, rows], level1_out, level1_in[s][r], at_axis(d, q))

    def level1_finish(s, r):
        rows = pl.ds(r, 1)
        arrived(dir2.at[s, :, rows], level1_in[s][r])
        at = where(s, rows, fixed_of(s, 2))
        v = [dir2[s, k, rows].astype(F32) for k in range(3)]
        v = ((part[at].astype(F32) + v[0]) + (v[1] + v[2])).astype(BF)
        d = ORDER[s][2]
        last_in[s, coord[d], rows] = v
        for k in (2, 1, 3):
            ref = last_in.at[s, coord[d], rows]
            send(ref, ref, last_out, last_sem[s][r], at_axis(d, lax.rem(coord[d] + k, 4)))

    def last_finish(s, r):
        rows = pl.ds(r, 1)
        arrived(last_in.at[s, pl.ds(0, 3), rows], last_sem[s][r])
        v = [last_in[s, k, rows].astype(F32) for k in range(4)]
        pilot[where(s, rows, fixed_of(s, 2))] = ((v[0] + v[1]) + (v[2] + v[3])).astype(BF)

    for r in range(4):
        v = dot(oh[1024 * r:1024 * (r + 1)], spec[...].reshape(2 * TR, HC)).astype(BF)
        for s in range(3):
            part[s, r] = v[:, 128 * s:128 * (s + 1)].reshape(4, 4, 4, 16, 128)
        for s in range(3):
            slab_send(s, r)

    lane = lax.broadcasted_iota(jnp.int32, (128, 128), 1)

    def other_one_hot(n):
        @pl.loop(2 * n, 2 * n + 2)
        def _(k):
            half = lax.div(k, 4)
            lanes = pl.ds(pl.multiple_of(lax.rem(k, 4) * 128, 128), 128)
            rows = pl.ds(pl.multiple_of(k * 128, 128), 128)
            col = jnp.transpose(jnp.broadcast_to(idxs[half, 0:1, lanes], (128, 128)))
            for n in range(NB // 128):
                oht[rows, 128 * n:128 * (n + 1)] = jnp.where(col == lane + 128 * n, 1.0, 0.0).astype(BF)
            col = jnp.transpose(jnp.broadcast_to(idxs[half, 1:2, lanes], (128, 128)))
            shot_one[rows] = jnp.where(col == lane, 1.0, 0.0).astype(BF)
            col = jnp.transpose(jnp.broadcast_to(idxs[half, 2:3, lanes], (128, 128)))
            for n in range(2):
                rcv_one[rows, 128 * n:128 * (n + 1)] = jnp.where(col == lane + 128 * n, 1.0, 0.0).astype(BF)

    for h in range(2):
        shots = lax.broadcasted_iota(jnp.int32, (SHOT_DEV, TR), 0)
        member[h, :SHOT_DEV] = jnp.where(shots == idxs[h, 1:2, :], 1.0, 0.0).astype(BF)
        rcvs = lax.broadcasted_iota(jnp.int32, (RCV_DEV, TR), 0)
        member[h, SHOT_DEV:] = jnp.where(rcvs == idxs[h, 2:3, :], 1.0, 0.0).astype(BF)

    ag0_out, ag1_out = new_sem(), new_sem()
    ag1_in = by_slab()
    ag_far = [[new_sem() for _ in range(4)] for _ in range(3)]
    ag_in = [new_sem() for _ in range(4)]

    def ag_slab(s, r, way):
        d = ORDER[s][0]
        ref = pilot.at[where(s, r, fixed_of(s, 1))]
        sem = ag_far[s][r] if way == r % 2 else ag_in[r]
        send(ref, ref, ag0_out, sem, at_axis(d, lax.rem(coord[d] + (1, 3)[way], 4)))

    def ag_forward(s, r):
        d = ORDER[s][0]
        way = r % 2
        ref = pilot.at[where(s, r, {d: lax.rem(coord[d] + (3, 1)[way], 4)})]
        arrived(ref, ag_far[s][r])
        send(ref, ref, ag0_out, ag_in[r], at_axis(d, lax.rem(coord[d] + (1, 3)[way], 4)))

    def gather_send(s, r):
        last_finish(s, r)
        d = ORDER[s][1]
        ref = pilot.at[where(s, pl.ds(r, 1), fixed_of(s, 2))]
        for k in (2, 1, 3):
            send(ref, ref, ag1_out, ag1_in[s][r], at_axis(d, lax.rem(coord[d] + k, 4)))

    def gather_slab(s, r):
        arrived(dir2.at[s, :, pl.ds(r, 1)], ag1_in[s][r])
        ag_slab(s, r, r % 2)
        ag_slab(s, r, 1 - r % 2)

    for n, step in enumerate((slab_forward, slab_finish, level1_finish, gather_send, gather_slab, ag_forward)):
        if n > 1:
            other_one_hot(n - 2)
        for r in range(4):
            for s in range(3):
                step(s, r)

    for r in range(4):
        arrived(part.at[:, 0, pl.ds(0, 2)], ag_in[r])
        v = dot(oht[:, 1024 * r:1024 * (r + 1)],
                jnp.concatenate([pilot[s, r].reshape(1024, 128) for s in range(3)], axis=1))
        if r == 0:
            cross[...] = v
        else:
            cross[...] += v

    low = low_half(128)

    @pl.loop(0, 8)
    def _(k):
        v = groups(cross[pl.ds(pl.multiple_of(k * 128, 128), 128)])
        p = jnp.sum(v[0] * v[0] + v[1] * v[1] + v[2] * v[2], axis=1, keepdims=True)
        power[c, pl.ds(k, 1)] = jnp.transpose(jnp.broadcast_to(p, (128, 128)))[0:1]

    p_copy = send(power.at[c], power.at[c], new_sem(), new_sem(), partner)

    @pl.loop(0, 8)
    def _(k):
        rows = pl.ds(pl.multiple_of(k * 128, 128), 128)
        inner = pl.ds(pl.multiple_of(lax.rem(k, 4) * 128, 128), 128)
        v = times_conj(groups(spec[lax.div(k, 4), inner].astype(F32)), groups(cross[rows]), low)
        for s in range(3):
            cross[rows, 128 * s:128 * (s + 1)] = v[s]

    def put_split(rows, v):
        for s in range(3):
            hi = v[s].astype(BF)
            high[rows, 128 * s:128 * (s + 1)] = hi
            rest[rows, 128 * s:128 * (s + 1)] = (v[s] - hi.astype(F32)).astype(BF)

    p_copy.wait()

    @pl.loop(0, 8)
    def _(k):
        rows = pl.ds(pl.multiple_of(k * 128, 128), 128)
        p = power[0, pl.ds(k, 1)] + power[1, pl.ds(k, 1)]
        scale = lax.rsqrt(jnp.transpose(jnp.broadcast_to(p, (128, 128))) / NF + 1e-06)
        v = [g * scale for g in groups(cross[rows])]
        for s in range(3):
            cross[rows, 128 * s:128 * (s + 1)] = v[s]
        put_split(rows, v)

    def soft(v):
        return jnp.concatenate(soften(groups(v)), axis=1).astype(BF)

    my_rcv = pl.ds(pl.multiple_of(i * 32, 32), 32)
    shots_sem = [(new_sem(), new_sem()) for _ in range(2)]
    rcvs_sem = [(new_sem(), new_sem()) for _ in range(2)]
    back_sem = [(new_sem(), new_sem()) for _ in range(2)]
    plane = [4 * lax.rem(z + kz, 4) + lax.rem(x + kx, 4) for kx, kz in FAR_FIRST]

    def shots_out(sweep):
        for k in (2, 1, 3):
            send(zs_st.at[sweep], zs_rv.at[sweep, y], *shots_sem[sweep], at_axis(1, lax.rem(y + k, 4)))
        zs_rv[sweep, y] = zs_st[sweep]

    def rcvs_out(sweep):
        for to in plane:
            rows = pl.ds(pl.multiple_of(to * 32, 32), 32)
            send(zr_st.at[sweep, rows], zr_rv.at[sweep, i], *rcvs_sem[sweep], (to, j))
        zr_rv[sweep, i] = zr_st[sweep, my_rcv]

    def shots_in(sweep):
        arrived(zs_rv.at[sweep, pl.ds(0, 3)], shots_sem[sweep][1])
        zs = zs_rv[sweep, 0].astype(F32)
        for k in range(1, 4):
            zs += zs_rv[sweep, k].astype(F32)
        shot_ph[sweep] = soft(zs)

    def rcvs_in(sweep):
        arrived(zr_rv.at[sweep, pl.ds(0, 15)], rcvs_sem[sweep][1])
        zr = zr_rv[sweep, 0].astype(F32)
        for k in range(1, 16):
            zr += zr_rv[sweep, k].astype(F32)
        return soft(zr)

    both = []
    for h in range(2):
        rows = slice(TR * h, TR * (h + 1))
        both.append(dot(member[h], high[rows]) + dot(member[h], rest[rows]))
        zr_st[0, RCV_DEV * h:RCV_DEV * (h + 1)] = both[h][SHOT_DEV:].astype(BF)
    zs_st[0] = (both[0][:SHOT_DEV] + both[1][:SHOT_DEV]).astype(BF)
    shots_out(0)
    rcvs_out(0)
    rcv_ph[0, my_rcv] = rcvs_in(0)
    ref = rcv_ph.at[0, my_rcv]
    for to in plane:
        send(ref, ref, *back_sem[0], (to, j))
    shots_in(0)

    def turned():
        @pl.loop(0, 8)
        def _(k):
            rows = pl.ds(pl.multiple_of(k * 128, 128), 128)
            put_split(rows, times_conj(groups(cross[rows]), groups(turn[rows]), low))

    turn[...] = dot(shot_one[...], shot_ph[0])
    turned()
    for h in range(2):
        rows = slice(TR * h, TR * (h + 1))
        m = member[h, SHOT_DEV:]
        zr_st[1, RCV_DEV * h:RCV_DEV * (h + 1)] = (dot(m, high[rows]) + dot(m, rest[rows])).astype(BF)
    rcvs_out(1)
    arrived(rcv_ph.at[0, pl.ds(0, 480)], back_sem[0][1])
    for h in range(2):
        rows = slice(TR * h, TR * (h + 1))
        turn[rows] = dot(rcv_one[rows], rcv_ph[0, RCV_DEV * h:RCV_DEV * (h + 1)])
    turned()
    zs = []
    for h in range(2):
        rows = slice(TR * h, TR * (h + 1))
        m = member[h, :SHOT_DEV]
        zs.append(dot(m, high[rows]) + dot(m, rest[rows]))
    zs_st[1] = (zs[0] + zs[1]).astype(BF)
    shots_out(1)

    rcv_ph[1, my_rcv] = rcvs_in(1)
    ref = rcv_ph.at[1, my_rcv]
    home = lax.div(i, 8)
    rows = pl.ds(pl.multiple_of(lax.rem(i, 8) * 32, 32), 32)
    for to in plane:
        send(ref, rcv_out.at[c, rows], *back_sem[1], (to, 2 * y + home))

    @pl.when(home == c)
    def _():
        rcv_out[c, rows] = rcv_ph[1, my_rcv]

    @pl.when(home != c)
    def _():
        send(ref, rcv_out.at[c, rows], *back_sem[1], partner)

    shots_in(1)
    last = send(shot_ph.at[1], shot_out.at[c], new_sem(), new_sem(), partner)
    shot_out[c] = shot_ph[1]
    sent(part.at[:, pl.ds(0, 3)], slabs_out)
    sent(dir2, level1_out)
    sent(last_in.at[:, pl.ds(0, 3)], last_out)
    sent(part.at[:, pl.ds(0, 3)], ag0_out)
    sent(dir2, ag1_out)
    for sweep in range(2):
        sent(zs_rv.at[sweep, pl.ds(0, 3)], shots_sem[sweep][0])
        sent(zr_rv.at[sweep, pl.ds(0, 15)], rcvs_sem[sweep][0])
    sent(rcv_ph.at[0, pl.ds(0, 480)], back_sem[0][0])
    last.wait()

    @pl.when(home == c)
    def _():
        sent(rcv_ph.at[1, pl.ds(0, 480)], back_sem[1][0])
        arrived(rcv_ph.at[1, pl.ds(0, 480)], back_sem[1][1])

    @pl.when(home != c)
    def _():
        sent(rcv_ph.at[1], back_sem[1][0])
        arrived(rcv_ph.at[1], back_sem[1][1])


def unpack(shots, rcvs, shot_out, rcv_out):
    for src, dst, n in ((shots, shot_out, SHOT_DEV), (rcvs, rcv_out, RCV_DEV)):
        mask = low_half(n)
        first, last = (groups(src[h].astype(F32)) for h in range(2))
        for part in range(2):
            dst[part, :, 0:128] = first[part]
            dst[part, :, 256:384] = last[part]
        dst[0, :, 128:256] = jnp.where(mask, first[2], swap(last[2]))
        dst[1, :, 128:256] = jnp.where(mask, swap(first[2]), last[2])


def shards(table, traces, cmp_bin, shot_index, rcv_index, live):
    vmem = pl.BlockSpec(memory_space=pltpu.VMEM)
    hbm = pl.BlockSpec(memory_space=pl.ANY)
    dma = pltpu.SemaphoreType.DMA
    packed = pl.pallas_call(
        kernel,
        out_shape=(
            jax.ShapeDtypeStruct((2, SHOT_DEV, HC), BF),
            jax.ShapeDtypeStruct((2, RCV_DEV, HC), BF),
        ),
        in_specs=[hbm] * 6,
        out_specs=(vmem, vmem),
        scratch_shapes=[
            pltpu.VMEM((NT, TR), BF),
            pltpu.VMEM((2, HC, NT), BF),
            pltpu.VMEM((4, 1, TR), jnp.int32),
            pltpu.VMEM((2, TR, HC), BF),
            pltpu.VMEM((TR, HC), BF),
            pltpu.VMEM((2, 8, TR), jnp.int32),
            pltpu.VMEM((NB, 2 * TR), BF),
            pltpu.VMEM((2 * TR, NB), BF),
            pltpu.VMEM((3, 4, 4, 4, 4, 16, 128), BF),
            pltpu.VMEM((3, 4, 4, 4, 4, 16, 128), BF),
            pltpu.VMEM((2 * TR, HC), F32),
            pltpu.VMEM((2 * TR, HC), F32),
            pltpu.VMEM((2 * TR, HC), BF),
            pltpu.VMEM((2 * TR, HC), BF),
            pltpu.VMEM((2, 8, 128), F32),
            pltpu.VMEM((2, SHOT_DEV + RCV_DEV, TR), BF),
            pltpu.VMEM((2 * TR, SHOT_DEV), BF),
            pltpu.VMEM((2 * TR, RCV_DEV), BF),
            pltpu.VMEM((2, SHOT_DEV, HC), BF),
            pltpu.VMEM((2, 2 * RCV_DEV, HC), BF),
            pltpu.VMEM((2, 4, SHOT_DEV, HC), BF),
            pltpu.VMEM((2, 16, 32, HC), BF),
            pltpu.VMEM((2, SHOT_DEV, HC), BF),
            pltpu.VMEM((2, 2 * RCV_DEV, HC), BF),
            pltpu.VMEM((3, 4, 4, 4, 16, 128), BF),
            pltpu.VMEM((3, 2, 4, 4, 4, 16, 128), BF),
            pltpu.VMEM((3, 3, 4, 4, 16, 128), BF),
            pltpu.VMEM((3, 4, 4, 4, 16, 128), BF),
            dma((112,)),
        ],
        compiler_params=pltpu.CompilerParams(
            collective_id=0, has_side_effects=True, vmem_limit_bytes=56 * 1024 * 1024
        ),
    )(traces.T, table, *(v.reshape(1, TR) for v in (cmp_bin, shot_index, rcv_index, live)))
    return pl.pallas_call(
        unpack,
        out_shape=(
            jax.ShapeDtypeStruct((2, SHOT_DEV, NF), F32),
            jax.ShapeDtypeStruct((2, RCV_DEV, NF), F32),
        ),
        in_specs=[vmem] * 2,
        out_specs=(vmem, vmem),
    )(*packed)


def solution(mesh):
    split = P(("shot", "rcv"))
    table = dft_halves()

    def run(traces, cmp_bin, shot_index, rcv_index, live):
        return jax.shard_map(
            shards,
            mesh=mesh,
            in_specs=(P(), P(("shot", "rcv"), None), split, split, split, split),
            out_specs=(P(None, "shot", None), P(None, "rcv", None)),
            check_vma=False,
        )(jnp.asarray(table), traces, cmp_bin, shot_index, rcv_index, live)

    return run
```

```python
import itertools
import math

import jax
import jax.numpy as jnp
import numpy as np
from jax import lax
from jax.experimental import pallas as pl
from jax.experimental.pallas import tpu as pltpu
from jax.sharding import PartitionSpec as P

NT = 2000
NF = 384
FLO = 20
SHOT_DEV = 128
RCV_DEV = 256
TR = 512
NB = 4096
HC = NF
MESH = pl.DeviceIdType.MESH
ORDER = ((0, 1, 2), (1, 2, 0), (2, 0, 1))
FAR_FIRST = ((2, 2), (3, 2), (2, 3), (2, 1), (1, 2), (3, 3), (3, 1), (2, 0), (1, 3), (1, 1), (0, 2), (3, 0), (1, 0), (0, 3), (0, 1))
BF = jnp.bfloat16
F32 = jnp.float32


def dft_halves():
    sample = np.arange(NT, dtype=np.int32)
    band = FLO + np.arange(NF, dtype=np.int32)
    angles = (band[:, None] * sample[None, :] % NT).astype(np.float32) * np.float32(2.0 * math.pi / NT)
    factor = np.float32(1.0 / math.sqrt(NT))
    re, im = np.cos(angles) * factor, -np.sin(angles) * factor
    halves = [np.concatenate([re[a:a + 128], im[a:a + 128], re[b:b + 64], im[b:b + 64]])
              for a, b in ((0, 128), (256, 192))]
    return np.stack(halves).astype(jnp.bfloat16)


def dot(a, b):
    return jnp.dot(a, b, preferred_element_type=F32)


def swap(v):
    return pltpu.roll(v, 64, axis=1)


def low_half(rows):
    return lax.broadcasted_iota(jnp.int32, (rows, 128), 1) < 64


def times_conj(a, b, low):
    same = a[2] * b[2]
    mixed = a[2] * swap(b[2])
    return (a[0] * b[0] + a[1] * b[1], a[1] * b[0] - a[0] * b[1],
            jnp.where(low, same + swap(same), mixed - swap(mixed)))


def soften(v):
    sq = [g * g for g in v]
    scale = lax.rsqrt(sq[0] + sq[1] + 1.0)
    return (v[0] * scale, v[1] * scale, v[2] * lax.rsqrt(sq[2] + swap(sq[2]) + 1.0))


def groups(v):
    return tuple(v[:, 128 * s:128 * (s + 1)] for s in range(3))


def kernel(traces_hbm, table_hbm, cmp_bin, shot_index, rcv_index, live, shot_out, rcv_out,
           traces, table, raw, spec, theirs, idxs, oh, oht, part, pilot, cross, turn, high, power, member, shot_one,
           rcv_one, zs_st, zr_st, zs_rv, zr_rv, shot_ph, rcv_ph, opp1, dir1, dir2, last_in, sems):
    i = lax.axis_index("shot")
    j = lax.axis_index("rcv")
    z, x = lax.div(i, 4), lax.rem(i, 4)
    y, c = lax.div(j, 2), lax.rem(j, 2)
    coord = (x, y, z)
    oc = 1 - c
    partner = (i, 2 * y + oc)
    numbers = itertools.count()

    def new_sem():
        return sems.at[next(numbers)]

    def at_axis(d, v):
        if d == 0:
            return (z * 4 + v, j)
        if d == 1:
            return (i, 2 * v + c)
        return (v * 4 + x, j)

    def fetch(src, dst, sem):
        copy = pltpu.make_async_copy(src, dst, sem)
        copy.start()
        return copy

    raw_sem, traces_sem = new_sem(), new_sem()
    for n, ref in enumerate((cmp_bin, shot_index, rcv_index, live)):
        fetch(ref, raw.at[n], raw_sem)
    for n in range(4):
        rows = pl.ds(512 * n, min(512, NT - 512 * n))
        fetch(traces_hbm.at[rows], traces.at[rows], traces_sem)
    table_in = [[fetch(table_hbm.at[h, pl.ds(128 * g, 128)], table.at[n, pl.ds(128 * g, 128)], new_sem())
                 for g in range(3)] for n, h in enumerate((oc, c))]

    barrier = pltpu.get_barrier_semaphore()
    for d in range(3):
        for k in (2, 1, 3):
            pl.semaphore_signal(barrier, inc=1, device_id=at_axis(d, lax.rem(coord[d] + k, 4)), device_id_type=MESH)
    pl.semaphore_signal(barrier, inc=1, device_id=partner, device_id_type=MESH)

    def send(src, dst, s_sem, r_sem, dev):
        copy = pltpu.make_async_remote_copy(src_ref=src, dst_ref=dst, send_sem=s_sem, recv_sem=r_sem, device_id=dev,
                                            device_id_type=MESH)
        copy.start()
        return copy

    def arrived(ref, sem):
        pltpu.make_async_remote_copy(src_ref=ref, dst_ref=ref, send_sem=sem, recv_sem=sem, device_id=partner,
                                     device_id_type=MESH).wait_recv()

    def sent(ref, sem):
        pltpu.make_async_remote_copy(src_ref=ref, dst_ref=ref, send_sem=sem, recv_sem=sem, device_id=partner,
                                     device_id_type=MESH).wait_send()

    pltpu.make_async_copy(raw, raw, raw_sem).wait()
    idxs[c, 0:1] = jnp.where(raw[3] != 0, raw[0], -1)
    idxs[c, 1:2] = raw[1] - i * SHOT_DEV
    idxs[c, 2:3] = raw[2] - j * RCV_DEV
    idxs[c, 3:8] = jnp.zeros((5, TR), jnp.int32)
    pltpu.make_async_copy(traces, traces, traces_sem).wait()

    def dft(n, dst):
        for g in range(3):
            table_in[n][g].wait()
            v = dot(table[n, 128 * g:128 * (g + 1)], traces[...])
            dst[:, 128 * g:128 * (g + 1)] = jnp.transpose(v).astype(BF)

    dft(0, theirs)
    pl.semaphore_wait(barrier, 10)
    idx_copy = send(idxs.at[c], idxs.at[c], new_sem(), new_sem(), partner)
    spec_copy = send(theirs, spec.at[c], new_sem(), new_sem(), partner)
    dft(1, spec.at[c])
    idx_copy.wait()

    bin_row = jnp.concatenate([idxs[0, 0:1, :], idxs[1, 0:1, :]], axis=1)

    @pl.loop(0, NB // 128)
    def _(k):
        bins = lax.broadcasted_iota(jnp.int32, (128, 2 * TR), 0) + k * 128
        oh[pl.ds(pl.multiple_of(k * 128, 128), 128)] = jnp.where(bins == bin_row, 1.0, 0.0).astype(BF)

    spec_copy.wait()

    def where(s, r, fixed):
        return (s, r) + tuple(fixed[d] if d in fixed else slice(None) for d in (2, 1, 0))

    def fixed_of(s, level):
        return {d: coord[d] for d in ORDER[s][:level]}

    def by_slab():
        return [[new_sem() for _ in range(4)] for _ in range(3)]

    slabs_out, level1_out, last_out = new_sem(), new_sem(), new_sem()
    far_in = [[new_sem() for _ in range(4)] for _ in range(3)]
    slabs_in, level1_in, last_sem = by_slab(), by_slab(), by_slab()

    def far_send(s, r):
        d = ORDER[s][0]
        near, far = lax.rem(coord[d] + (1 if r % 2 == 0 else 3), 4), lax.rem(coord[d] + 2, 4)
        send(part.at[where(s, r, {d: far})], opp1.at[s, r], slabs_out, far_in[s][r], at_axis(d, near))

    def away_send(s, r):
        d = ORDER[s][0]
        away = lax.rem(coord[d] + (3 if r % 2 == 0 else 1), 4)
        send(part.at[where(s, r, {d: away})], dir1.at[s, r % 2, r], slabs_out, slabs_in[s][r], at_axis(d, away))

    def slab_forward(s, r):
        d = ORDER[s][0]
        near = lax.rem(coord[d] + (1 if r % 2 == 0 else 3), 4)
        arrived(opp1.at[s, r], far_in[s][r])
        at = where(s, r, {d: near})
        part[at] = (part[at].astype(F32) + opp1[s, r].astype(F32)).astype(BF)
        send(part.at[at], dir1.at[s, 1 - r % 2, r], slabs_out, slabs_in[s][r], at_axis(d, near))

    def slab_finish(s, r):
        arrived(dir1.at[s, :, pl.ds(r, 1)], slabs_in[s][r])
        at = where(s, pl.ds(r, 1), fixed_of(s, 1))
        rows = pl.ds(r, 1)
        part[at] = (part[at].astype(F32) + dir1[s, 0, rows].astype(F32) + dir1[s, 1, rows].astype(F32)).astype(BF)
        d = ORDER[s][1]
        for k in (2, 1, 3):
            q = lax.rem(coord[d] + k, 4)
            src = part.at[where(s, rows, {**fixed_of(s, 1), d: q})]
            send(src, dir2.at[s, k - 1, rows], level1_out, level1_in[s][r], at_axis(d, q))

    def level1_finish(s, r):
        rows = pl.ds(r, 1)
        arrived(dir2.at[s, :, rows], level1_in[s][r])
        at = where(s, rows, fixed_of(s, 2))
        v = [dir2[s, k, rows].astype(F32) for k in range(3)]
        v = ((part[at].astype(F32) + v[0]) + (v[1] + v[2])).astype(BF)
        d = ORDER[s][2]
        last_in[s, coord[d], rows] = v
        for k in (2, 1, 3):
            ref = last_in.at[s, coord[d], rows]
            send(ref, ref, last_out, last_sem[s][r], at_axis(d, lax.rem(coord[d] + k, 4)))

    def last_finish(s, r):
        rows = pl.ds(r, 1)
        arrived(last_in.at[s, pl.ds(0, 3), rows], last_sem[s][r])
        v = [last_in[s, k, rows].astype(F32) for k in range(4)]
        pilot[where(s, rows, fixed_of(s, 2))] = ((v[0] + v[1]) + (v[2] + v[3])).astype(BF)

    for r in range(4):
        v = dot(oh[1024 * r:1024 * (r + 1)], spec[...].reshape(2 * TR, HC)).astype(BF)
        for s in range(3):
            part[s, r] = v[:, 128 * s:128 * (s + 1)].reshape(4, 4, 4, 16, 128)
        for s in range(3):
            far_send(s, r)
        for s in range(3):
            away_send(s, r)

    lane = lax.broadcasted_iota(jnp.int32, (128, 128), 1)

    def other_one_hot(n):
        @pl.loop(2 * n, 2 * n + 2)
        def _(k):
            half = lax.div(k, 4)
            lanes = pl.ds(pl.multiple_of(lax.rem(k, 4) * 128, 128), 128)
            rows = pl.ds(pl.multiple_of(k * 128, 128), 128)
            col = jnp.transpose(jnp.broadcast_to(idxs[half, 0:1, lanes], (128, 128)))
            for n in range(NB // 128):
                oht[rows, 128 * n:128 * (n + 1)] = jnp.where(col == lane + 128 * n, 1.0, 0.0).astype(BF)
            col = jnp.transpose(jnp.broadcast_to(idxs[half, 1:2, lanes], (128, 128)))
            shot_one[rows] = jnp.where(col == lane, 1.0, 0.0).astype(BF)
            col = jnp.transpose(jnp.broadcast_to(idxs[half, 2:3, lanes], (128, 128)))
            for n in range(2):
                rcv_one[rows, 128 * n:128 * (n + 1)] = jnp.where(col == lane + 128 * n, 1.0, 0.0).astype(BF)

    for h in range(2):
        shots = lax.broadcasted_iota(jnp.int32, (SHOT_DEV, TR), 0)
        member[h, :SHOT_DEV] = jnp.where(shots == idxs[h, 1:2, :], 1.0, 0.0).astype(BF)
        rcvs = lax.broadcasted_iota(jnp.int32, (RCV_DEV, TR), 0)
        member[h, SHOT_DEV:] = jnp.where(rcvs == idxs[h, 2:3, :], 1.0, 0.0).astype(BF)

    ag0_out, ag1_out = new_sem(), new_sem()
    ag1_in = by_slab()
    ag_far = [[new_sem() for _ in range(4)] for _ in range(3)]
    ag_in = [new_sem() for _ in range(4)]

    def ag_slab(s, r, way):
        d = ORDER[s][0]
        ref = pilot.at[where(s, r, fixed_of(s, 1))]
        sem = ag_far[s][r] if way == r % 2 else ag_in[r]
        send(ref, ref, ag0_out, sem, at_axis(d, lax.rem(coord[d] + (1, 3)[way], 4)))

    def ag_forward(s, r):
        d = ORDER[s][0]
        way = r % 2
        ref = pilot.at[where(s, r, {d: lax.rem(coord[d] + (3, 1)[way], 4)})]
        arrived(ref, ag_far[s][r])
        send(ref, ref, ag0_out, ag_in[r], at_axis(d, lax.rem(coord[d] + (1, 3)[way], 4)))

    def gather_send(s, r):
        last_finish(s, r)
        d = ORDER[s][1]
        ref = pilot.at[where(s, pl.ds(r, 1), fixed_of(s, 2))]
        for k in (2, 1, 3):
            send(ref, ref, ag1_out, ag1_in[s][r], at_axis(d, lax.rem(coord[d] + k, 4)))

    def gather_slab(s, r):
        arrived(dir2.at[s, :, pl.ds(r, 1)], ag1_in[s][r])
        ag_slab(s, r, r % 2)
        ag_slab(s, r, 1 - r % 2)

    for n, step in enumerate((slab_forward, slab_finish, level1_finish, gather_send, gather_slab, ag_forward)):
        if n > 1:
            other_one_hot(n - 2)
        for r in range(4):
            for s in range(3):
                step(s, r)

    for r in range(4):
        arrived(part.at[:, 0, pl.ds(0, 2)], ag_in[r])
        v = dot(oht[:, 1024 * r:1024 * (r + 1)],
                jnp.concatenate([pilot[s, r].reshape(1024, 128) for s in range(3)], axis=1))
        if r == 0:
            cross[...] = v
        else:
            cross[...] += v

    low = low_half(128)

    @pl.loop(0, 8)
    def _(k):
        v = groups(cross[pl.ds(pl.multiple_of(k * 128, 128), 128)])
        p = jnp.sum(v[0] * v[0] + v[1] * v[1] + v[2] * v[2], axis=1, keepdims=True)
        power[c, pl.ds(k, 1)] = jnp.transpose(jnp.broadcast_to(p, (128, 128)))[0:1]

    p_copy = send(power.at[c], power.at[c], new_sem(), new_sem(), partner)

    @pl.loop(0, 8)
    def _(k):
        rows = pl.ds(pl.multiple_of(k * 128, 128), 128)
        inner = pl.ds(pl.multiple_of(lax.rem(k, 4) * 128, 128), 128)
        v = times_conj(groups(spec[lax.div(k, 4), inner].astype(F32)), groups(cross[rows]), low)
        for s in range(3):
            cross[rows, 128 * s:128 * (s + 1)] = v[s]

    def put_high(rows, v):
        for s in range(3):
            high[rows, 128 * s:128 * (s + 1)] = v[s].astype(BF)

    p_copy.wait()

    @pl.loop(0, 8)
    def _(k):
        rows = pl.ds(pl.multiple_of(k * 128, 128), 128)
        p = power[0, pl.ds(k, 1)] + power[1, pl.ds(k, 1)]
        scale = lax.rsqrt(jnp.transpose(jnp.broadcast_to(p, (128, 128))) / NF + 1e-06)
        v = [g * scale for g in groups(cross[rows])]
        for s in range(3):
            cross[rows, 128 * s:128 * (s + 1)] = v[s]
        put_high(rows, v)

    def soft(v):
        return jnp.concatenate(soften(groups(v)), axis=1).astype(BF)

    my_rcv = pl.ds(pl.multiple_of(i * 32, 32), 32)
    shots_sem = [(new_sem(), new_sem()) for _ in range(2)]
    rcvs_sem = [(new_sem(), new_sem()) for _ in range(2)]
    back_sem = [(new_sem(), new_sem()) for _ in range(2)]
    plane = [4 * lax.rem(z + kz, 4) + lax.rem(x + kx, 4) for kx, kz in FAR_FIRST]

    def shots_out(sweep):
        for k in (2, 1, 3):
            send(zs_st.at[sweep], zs_rv.at[sweep, y], *shots_sem[sweep], at_axis(1, lax.rem(y + k, 4)))
        zs_rv[sweep, y] = zs_st[sweep]

    def rcvs_out(sweep):
        for to in plane:
            rows = pl.ds(pl.multiple_of(to * 32, 32), 32)
            send(zr_st.at[sweep, rows], zr_rv.at[sweep, i], *rcvs_sem[sweep], (to, j))
        zr_rv[sweep, i] = zr_st[sweep, my_rcv]

    def shots_in(sweep):
        arrived(zs_rv.at[sweep, pl.ds(0, 3)], shots_sem[sweep][1])
        zs = zs_rv[sweep, 0].astype(F32)
        for k in range(1, 4):
            zs += zs_rv[sweep, k].astype(F32)
        shot_ph[sweep] = soft(zs)

    def rcvs_in(sweep):
        arrived(zr_rv.at[sweep, pl.ds(0, 15)], rcvs_sem[sweep][1])
        zr = zr_rv[sweep, 0].astype(F32)
        for k in range(1, 16):
            zr += zr_rv[sweep, k].astype(F32)
        return soft(zr)

    both = []
    for h in range(2):
        rows = slice(TR * h, TR * (h + 1))
        both.append(dot(member[h], high[rows]) )
        zr_st[0, RCV_DEV * h:RCV_DEV * (h + 1)] = both[h][SHOT_DEV:].astype(BF)
    zs_st[0] = (both[0][:SHOT_DEV] + both[1][:SHOT_DEV]).astype(BF)
    shots_out(0)
    rcvs_out(0)
    rcv_ph[0, my_rcv] = rcvs_in(0)
    ref = rcv_ph.at[0, my_rcv]
    for to in plane:
        send(ref, ref, *back_sem[0], (to, j))
    shots_in(0)

    def turned():
        @pl.loop(0, 8)
        def _(k):
            rows = pl.ds(pl.multiple_of(k * 128, 128), 128)
            put_high(rows, times_conj(groups(cross[rows]), groups(turn[rows]), low))

    turn[...] = dot(shot_one[...], shot_ph[0])
    turned()
    for h in range(2):
        rows = slice(TR * h, TR * (h + 1))
        m = member[h, SHOT_DEV:]
        zr_st[1, RCV_DEV * h:RCV_DEV * (h + 1)] = (dot(m, high[rows])).astype(BF)
    rcvs_out(1)
    arrived(rcv_ph.at[0, pl.ds(0, 480)], back_sem[0][1])
    for h in range(2):
        rows = slice(TR * h, TR * (h + 1))
        turn[rows] = dot(rcv_one[rows], rcv_ph[0, RCV_DEV * h:RCV_DEV * (h + 1)])
    turned()
    zs = []
    for h in range(2):
        rows = slice(TR * h, TR * (h + 1))
        m = member[h, :SHOT_DEV]
        zs.append(dot(m, high[rows]))
    zs_st[1] = (zs[0] + zs[1]).astype(BF)
    shots_out(1)

    rcv_ph[1, my_rcv] = rcvs_in(1)
    ref = rcv_ph.at[1, my_rcv]
    home = lax.div(i, 8)
    rows = pl.ds(pl.multiple_of(lax.rem(i, 8) * 32, 32), 32)
    for to in plane:
        send(ref, rcv_out.at[c, rows], *back_sem[1], (to, 2 * y + home))

    @pl.when(home == c)
    def _():
        rcv_out[c, rows] = rcv_ph[1, my_rcv]

    @pl.when(home != c)
    def _():
        send(ref, rcv_out.at[c, rows], *back_sem[1], partner)

    shots_in(1)
    last = send(shot_ph.at[1], shot_out.at[c], new_sem(), new_sem(), partner)
    shot_out[c] = shot_ph[1]
    sent(part.at[:, pl.ds(0, 3)], slabs_out)
    sent(dir2, level1_out)
    sent(last_in.at[:, pl.ds(0, 3)], last_out)
    sent(part.at[:, pl.ds(0, 3)], ag0_out)
    sent(dir2, ag1_out)
    for sweep in range(2):
        sent(zs_rv.at[sweep, pl.ds(0, 3)], shots_sem[sweep][0])
        sent(zr_rv.at[sweep, pl.ds(0, 15)], rcvs_sem[sweep][0])
    sent(rcv_ph.at[0, pl.ds(0, 480)], back_sem[0][0])
    last.wait()

    @pl.when(home == c)
    def _():
        sent(rcv_ph.at[1, pl.ds(0, 480)], back_sem[1][0])
        arrived(rcv_ph.at[1, pl.ds(0, 480)], back_sem[1][1])

    @pl.when(home != c)
    def _():
        sent(rcv_ph.at[1], back_sem[1][0])
        arrived(rcv_ph.at[1], back_sem[1][1])


def unpack(shots, rcvs, shot_out, rcv_out):
    for src, dst, n in ((shots, shot_out, SHOT_DEV), (rcvs, rcv_out, RCV_DEV)):
        mask = low_half(n)
        first, last = (groups(src[h].astype(F32)) for h in range(2))
        for part in range(2):
            dst[part, :, 0:128] = first[part]
            dst[part, :, 256:384] = last[part]
        dst[0, :, 128:256] = jnp.where(mask, first[2], swap(last[2]))
        dst[1, :, 128:256] = jnp.where(mask, swap(first[2]), last[2])


def shards(table, traces, cmp_bin, shot_index, rcv_index, live):
    vmem = pl.BlockSpec(memory_space=pltpu.VMEM)
    hbm = pl.BlockSpec(memory_space=pl.ANY)
    dma = pltpu.SemaphoreType.DMA
    packed = pl.pallas_call(
        kernel,
        out_shape=(
            jax.ShapeDtypeStruct((2, SHOT_DEV, HC), BF),
            jax.ShapeDtypeStruct((2, RCV_DEV, HC), BF),
        ),
        in_specs=[hbm] * 6,
        out_specs=(vmem, vmem),
        scratch_shapes=[
            pltpu.VMEM((NT, TR), BF),
            pltpu.VMEM((2, HC, NT), BF),
            pltpu.VMEM((4, 1, TR), jnp.int32),
            pltpu.VMEM((2, TR, HC), BF),
            pltpu.VMEM((TR, HC), BF),
            pltpu.VMEM((2, 8, TR), jnp.int32),
            pltpu.VMEM((NB, 2 * TR), BF),
            pltpu.VMEM((2 * TR, NB), BF),
            pltpu.VMEM((3, 4, 4, 4, 4, 16, 128), BF),
            pltpu.VMEM((3, 4, 4, 4, 4, 16, 128), BF),
            pltpu.VMEM((2 * TR, HC), F32),
            pltpu.VMEM((2 * TR, HC), F32),
            pltpu.VMEM((2 * TR, HC), BF),
            pltpu.VMEM((2, 8, 128), F32),
            pltpu.VMEM((2, SHOT_DEV + RCV_DEV, TR), BF),
            pltpu.VMEM((2 * TR, SHOT_DEV), BF),
            pltpu.VMEM((2 * TR, RCV_DEV), BF),
            pltpu.VMEM((2, SHOT_DEV, HC), BF),
            pltpu.VMEM((2, 2 * RCV_DEV, HC), BF),
            pltpu.VMEM((2, 4, SHOT_DEV, HC), BF),
            pltpu.VMEM((2, 16, 32, HC), BF),
            pltpu.VMEM((2, SHOT_DEV, HC), BF),
            pltpu.VMEM((2, 2 * RCV_DEV, HC), BF),
            pltpu.VMEM((3, 4, 4, 4, 16, 128), BF),
            pltpu.VMEM((3, 2, 4, 4, 4, 16, 128), BF),
            pltpu.VMEM((3, 3, 4, 4, 16, 128), BF),
            pltpu.VMEM((3, 4, 4, 4, 16, 128), BF),
            dma((112,)),
        ],
        compiler_params=pltpu.CompilerParams(
            collective_id=0, has_side_effects=True, vmem_limit_bytes=56 * 1024 * 1024
        ),
    )(traces.T, table, *(v.reshape(1, TR) for v in (cmp_bin, shot_index, rcv_index, live)))
    return pl.pallas_call(
        unpack,
        out_shape=(
            jax.ShapeDtypeStruct((2, SHOT_DEV, NF), F32),
            jax.ShapeDtypeStruct((2, RCV_DEV, NF), F32),
        ),
        in_specs=[vmem] * 2,
        out_specs=(vmem, vmem),
    )(*packed)


def solution(mesh):
    split = P(("shot", "rcv"))
    table = dft_halves()

    def run(traces, cmp_bin, shot_index, rcv_index, live):
        return jax.shard_map(
            shards,
            mesh=mesh,
            in_specs=(P(), P(("shot", "rcv"), None), split, split, split, split),
            out_specs=(P(None, "shot", None), P(None, "rcv", None)),
            check_vma=False,
        )(jnp.asarray(table), traces, cmp_bin, shot_index, rcv_index, live)

    return run
```

```python
import itertools
import math

import jax
import jax.numpy as jnp
import numpy as np
from jax import lax
from jax.experimental import pallas as pl
from jax.experimental.pallas import tpu as pltpu
from jax.sharding import PartitionSpec as P

NT = 2000
NF = 384
FLO = 20
SHOT_DEV = 128
RCV_DEV = 256
TR = 512
NB = 4096
HC = NF
MESH = pl.DeviceIdType.MESH
ORDER = ((0, 1, 2), (1, 2, 0), (2, 0, 1))
FAR_FIRST = ((2, 2), (3, 2), (2, 3), (2, 1), (1, 2), (3, 3), (3, 1), (2, 0), (1, 3), (1, 1), (0, 2), (3, 0), (1, 0), (0, 3), (0, 1))
BF = jnp.bfloat16
F32 = jnp.float32


def dft_halves():
    sample = np.arange(NT, dtype=np.int32)
    band = FLO + np.arange(NF, dtype=np.int32)
    angles = (band[:, None] * sample[None, :] % NT).astype(np.float32) * np.float32(2.0 * math.pi / NT)
    factor = np.float32(1.0 / math.sqrt(NT))
    re, im = np.cos(angles) * factor, -np.sin(angles) * factor
    halves = [np.concatenate([re[a:a + 128], im[a:a + 128], re[b:b + 64], im[b:b + 64]])
              for a, b in ((0, 128), (256, 192))]
    return np.stack(halves).astype(jnp.bfloat16)


def dot(a, b):
    return jnp.dot(a, b, preferred_element_type=F32)


def swap(v):
    return pltpu.roll(v, 64, axis=1)


def low_half(rows):
    return lax.broadcasted_iota(jnp.int32, (rows, 128), 1) < 64


def times_conj(a, b, low):
    same = a[2] * b[2]
    mixed = a[2] * swap(b[2])
    return (a[0] * b[0] + a[1] * b[1], a[1] * b[0] - a[0] * b[1],
            jnp.where(low, same + swap(same), mixed - swap(mixed)))


def soften(v):
    sq = [g * g for g in v]
    scale = lax.rsqrt(sq[0] + sq[1] + 1.0)
    return (v[0] * scale, v[1] * scale, v[2] * lax.rsqrt(sq[2] + swap(sq[2]) + 1.0))


def groups(v):
    return tuple(v[:, 128 * s:128 * (s + 1)] for s in range(3))


def kernel(traces_hbm, table_hbm, cmp_bin, shot_index, rcv_index, live, shot_out, rcv_out,
           traces, table, raw, spec, theirs, idxs, oh, oht, part, pilot, cross, turn, high, power, member, shot_one,
           rcv_one, zs_st, zr_st, zs_rv, zr_rv, shot_ph, rcv_ph, opp1, dir1, dir2, last_in, sems):
    i = lax.axis_index("shot")
    j = lax.axis_index("rcv")
    z, x = lax.div(i, 4), lax.rem(i, 4)
    y, c = lax.div(j, 2), lax.rem(j, 2)
    coord = (x, y, z)
    oc = 1 - c
    partner = (i, 2 * y + oc)
    numbers = itertools.count()

    def new_sem():
        return sems.at[next(numbers)]

    def at_axis(d, v):
        if d == 0:
            return (z * 4 + v, j)
        if d == 1:
            return (i, 2 * v + c)
        return (v * 4 + x, j)

    def fetch(src, dst, sem):
        copy = pltpu.make_async_copy(src, dst, sem)
        copy.start()
        return copy

    raw_sem, traces_sem = new_sem(), new_sem()
    for n, ref in enumerate((cmp_bin, shot_index, rcv_index, live)):
        fetch(ref, raw.at[n], raw_sem)
    for n in range(4):
        rows = pl.ds(512 * n, min(512, NT - 512 * n))
        fetch(traces_hbm.at[rows], traces.at[rows], traces_sem)
    table_in = [[fetch(table_hbm.at[h, pl.ds(128 * g, 128)], table.at[n, pl.ds(128 * g, 128)], new_sem())
                 for g in range(3)] for n, h in enumerate((oc, c))]

    barrier = pltpu.get_barrier_semaphore()
    for d in range(3):
        for k in (1, 3):
            pl.semaphore_signal(barrier, inc=1, device_id=at_axis(d, lax.rem(coord[d] + k, 4)), device_id_type=MESH)
    pl.semaphore_signal(barrier, inc=1, device_id=partner, device_id_type=MESH)

    def send(src, dst, s_sem, r_sem, dev):
        copy = pltpu.make_async_remote_copy(src_ref=src, dst_ref=dst, send_sem=s_sem, recv_sem=r_sem, device_id=dev,
                                            device_id_type=MESH)
        copy.start()
        return copy

    def arrived(ref, sem):
        pltpu.make_async_remote_copy(src_ref=ref, dst_ref=ref, send_sem=sem, recv_sem=sem, device_id=partner,
                                     device_id_type=MESH).wait_recv()

    def sent(ref, sem):
        pltpu.make_async_remote_copy(src_ref=ref, dst_ref=ref, send_sem=sem, recv_sem=sem, device_id=partner,
                                     device_id_type=MESH).wait_send()

    pltpu.make_async_copy(raw, raw, raw_sem).wait()
    idxs[c, 0:1] = jnp.where(raw[3] != 0, raw[0], -1)
    idxs[c, 1:2] = raw[1] - i * SHOT_DEV
    idxs[c, 2:3] = raw[2] - j * RCV_DEV
    idxs[c, 3:8] = jnp.zeros((5, TR), jnp.int32)
    pltpu.make_async_copy(traces, traces, traces_sem).wait()

    def dft(n, dst):
        for g in range(3):
            table_in[n][g].wait()
            v = dot(table[n, 128 * g:128 * (g + 1)], traces[...])
            dst[:, 128 * g:128 * (g + 1)] = jnp.transpose(v).astype(BF)

    dft(0, theirs)
    pl.semaphore_wait(barrier, 7)
    idx_copy = send(idxs.at[c], idxs.at[c], new_sem(), new_sem(), partner)
    spec_copy = send(theirs, spec.at[c], new_sem(), new_sem(), partner)
    dft(1, spec.at[c])
    idx_copy.wait()

    bin_row = jnp.concatenate([idxs[0, 0:1, :], idxs[1, 0:1, :]], axis=1)

    @pl.loop(0, NB // 128)
    def _(k):
        bins = lax.broadcasted_iota(jnp.int32, (128, 2 * TR), 0) + k * 128
        oh[pl.ds(pl.multiple_of(k * 128, 128), 128)] = jnp.where(bins == bin_row, 1.0, 0.0).astype(BF)

    spec_copy.wait()

    def where(s, r, fixed):
        return (s, r) + tuple(fixed[d] if d in fixed else slice(None) for d in (2, 1, 0))

    def fixed_of(s, level):
        return {d: coord[d] for d in ORDER[s][:level]}

    def by_slab():
        return [[new_sem() for _ in range(4)] for _ in range(3)]

    slabs_out, level1_out, last_out = new_sem(), new_sem(), new_sem()
    far_in = [[new_sem() for _ in range(4)] for _ in range(3)]
    slabs_in, level1_in, last_sem = by_slab(), by_slab(), by_slab()

    def far_send(s, r):
        d = ORDER[s][0]
        near, far = lax.rem(coord[d] + (1 if r % 2 == 0 else 3), 4), lax.rem(coord[d] + 2, 4)
        send(part.at[where(s, r, {d: far})], opp1.at[s, r], slabs_out, far_in[s][r], at_axis(d, near))

    def away_send(s, r):
        d = ORDER[s][0]
        away = lax.rem(coord[d] + (3 if r % 2 == 0 else 1), 4)
        send(part.at[where(s, r, {d: away})], dir1.at[s, r % 2, r], slabs_out, slabs_in[s][r], at_axis(d, away))

    def slab_forward(s, r):
        d = ORDER[s][0]
        near = lax.rem(coord[d] + (1 if r % 2 == 0 else 3), 4)
        arrived(opp1.at[s, r], far_in[s][r])
        at = where(s, r, {d: near})
        part[at] = (part[at].astype(F32) + opp1[s, r].astype(F32)).astype(BF)
        send(part.at[at], dir1.at[s, 1 - r % 2, r], slabs_out, slabs_in[s][r], at_axis(d, near))

    def slab_finish(s, r):
        arrived(dir1.at[s, :, pl.ds(r, 1)], slabs_in[s][r])
        at = where(s, pl.ds(r, 1), fixed_of(s, 1))
        rows = pl.ds(r, 1)
        part[at] = (part[at].astype(F32) + dir1[s, 0, rows].astype(F32) + dir1[s, 1, rows].astype(F32)).astype(BF)
        d = ORDER[s][1]
        for k in (2, 1, 3):
            q = lax.rem(coord[d] + k, 4)
            src = part.at[where(s, rows, {**fixed_of(s, 1), d: q})]
            send(src, dir2.at[s, k - 1, rows], level1_out, level1_in[s][r], at_axis(d, q))

    def level1_finish(s, r):
        rows = pl.ds(r, 1)
        arrived(dir2.at[s, :, rows], level1_in[s][r])
        at = where(s, rows, fixed_of(s, 2))
        v = [dir2[s, k, rows].astype(F32) for k in range(3)]
        v = ((part[at].astype(F32) + v[0]) + (v[1] + v[2])).astype(BF)
        d = ORDER[s][2]
        last_in[s, coord[d], rows] = v
        for k in (2, 1, 3):
            ref = last_in.at[s, coord[d], rows]
            send(ref, ref, last_out, last_sem[s][r], at_axis(d, lax.rem(coord[d] + k, 4)))

    def last_finish(s, r):
        rows = pl.ds(r, 1)
        arrived(last_in.at[s, pl.ds(0, 3), rows], last_sem[s][r])
        v = [last_in[s, k, rows].astype(F32) for k in range(4)]
        pilot[where(s, rows, fixed_of(s, 2))] = ((v[0] + v[1]) + (v[2] + v[3])).astype(BF)

    for r in range(4):
        v = dot(oh[1024 * r:1024 * (r + 1)], spec[...].reshape(2 * TR, HC)).astype(BF)
        for s in range(3):
            part[s, r] = v[:, 128 * s:128 * (s + 1)].reshape(4, 4, 4, 16, 128)
        for s in range(3):
            far_send(s, r)
        for s in range(3):
            away_send(s, r)

    lane = lax.broadcasted_iota(jnp.int32, (128, 128), 1)

    def other_one_hot(n):
        @pl.loop(2 * n, 2 * n + 2)
        def _(k):
            half = lax.div(k, 4)
            lanes = pl.ds(pl.multiple_of(lax.rem(k, 4) * 128, 128), 128)
            rows = pl.ds(pl.multiple_of(k * 128, 128), 128)
            col = jnp.transpose(jnp.broadcast_to(idxs[half, 0:1, lanes], (128, 128)))
            for n in range(NB // 128):
                oht[rows, 128 * n:128 * (n + 1)] = jnp.where(col == lane + 128 * n, 1.0, 0.0).astype(BF)
            col = jnp.transpose(jnp.broadcast_to(idxs[half, 1:2, lanes], (128, 128)))
            shot_one[rows] = jnp.where(col == lane, 1.0, 0.0).astype(BF)
            col = jnp.transpose(jnp.broadcast_to(idxs[half, 2:3, lanes], (128, 128)))
            for n in range(2):
                rcv_one[rows, 128 * n:128 * (n + 1)] = jnp.where(col == lane + 128 * n, 1.0, 0.0).astype(BF)

    def members():
        for h in range(2):
            shots = lax.broadcasted_iota(jnp.int32, (SHOT_DEV, TR), 0)
            member[h, :SHOT_DEV] = jnp.where(shots == idxs[h, 1:2, :], 1.0, 0.0).astype(BF)
            rcvs = lax.broadcasted_iota(jnp.int32, (RCV_DEV, TR), 0)
            member[h, SHOT_DEV:] = jnp.where(rcvs == idxs[h, 2:3, :], 1.0, 0.0).astype(BF)

    ag0_out, ag1_out = new_sem(), new_sem()
    ag1_in = by_slab()
    ag_far = [[new_sem() for _ in range(4)] for _ in range(3)]
    ag_in = [new_sem() for _ in range(4)]

    def ag_slab(s, r, way):
        d = ORDER[s][0]
        ref = pilot.at[where(s, r, fixed_of(s, 1))]
        sem = ag_far[s][r] if way == r % 2 else ag_in[r]
        send(ref, ref, ag0_out, sem, at_axis(d, lax.rem(coord[d] + (1, 3)[way], 4)))

    def ag_forward(s, r):
        d = ORDER[s][0]
        way = r % 2
        ref = pilot.at[where(s, r, {d: lax.rem(coord[d] + (3, 1)[way], 4)})]
        arrived(ref, ag_far[s][r])
        send(ref, ref, ag0_out, ag_in[r], at_axis(d, lax.rem(coord[d] + (1, 3)[way], 4)))

    def gather_send(s, r):
        last_finish(s, r)
        d = ORDER[s][1]
        ref = pilot.at[where(s, pl.ds(r, 1), fixed_of(s, 2))]
        for k in (2, 1, 3):
            send(ref, ref, ag1_out, ag1_in[s][r], at_axis(d, lax.rem(coord[d] + k, 4)))

    def gather_slab(s, r):
        arrived(dir2.at[s, :, pl.ds(r, 1)], ag1_in[s][r])
        ag_slab(s, r, r % 2)
        ag_slab(s, r, 1 - r % 2)

    for n, step in enumerate((slab_forward, slab_finish, level1_finish, gather_send, gather_slab, ag_forward)):
        if n > 1:
            other_one_hot(n - 2)
        if n == 5:
            members()
        for r in range(4):
            for s in range(3):
                step(s, r)

    for r in range(4):
        arrived(part.at[:, 0, pl.ds(0, 2)], ag_in[r])
        v = dot(oht[:, 1024 * r:1024 * (r + 1)],
                jnp.concatenate([pilot[s, r].reshape(1024, 128) for s in range(3)], axis=1))
        if r == 0:
            cross[...] = v
        else:
            cross[...] += v

    low = low_half(128)

    @pl.loop(0, 8)
    def _(k):
        v = groups(cross[pl.ds(pl.multiple_of(k * 128, 128), 128)])
        p = jnp.sum(v[0] * v[0] + v[1] * v[1] + v[2] * v[2], axis=1, keepdims=True)
        power[c, pl.ds(k, 1)] = jnp.transpose(jnp.broadcast_to(p, (128, 128)))[0:1]

    p_copy = send(power.at[c], power.at[c], new_sem(), new_sem(), partner)

    @pl.loop(0, 8)
    def _(k):
        rows = pl.ds(pl.multiple_of(k * 128, 128), 128)
        inner = pl.ds(pl.multiple_of(lax.rem(k, 4) * 128, 128), 128)
        v = times_conj(groups(spec[lax.div(k, 4), inner].astype(F32)), groups(cross[rows]), low)
        for s in range(3):
            cross[rows, 128 * s:128 * (s + 1)] = v[s]

    def put_high(rows, v):
        for s in range(3):
            high[rows, 128 * s:128 * (s + 1)] = v[s].astype(BF)

    p_copy.wait()

    @pl.loop(0, 8)
    def _(k):
        rows = pl.ds(pl.multiple_of(k * 128, 128), 128)
        p = power[0, pl.ds(k, 1)] + power[1, pl.ds(k, 1)]
        scale = lax.rsqrt(jnp.transpose(jnp.broadcast_to(p, (128, 128))) / NF + 1e-06)
        v = [g * scale for g in groups(cross[rows])]
        for s in range(3):
            cross[rows, 128 * s:128 * (s + 1)] = v[s]
        put_high(rows, v)

    def soft(v):
        return jnp.concatenate(soften(groups(v)), axis=1).astype(BF)

    my_rcv = pl.ds(pl.multiple_of(i * 32, 32), 32)
    shots_sem = [(new_sem(), new_sem()) for _ in range(2)]
    rcvs_sem = [(new_sem(), new_sem()) for _ in range(2)]
    back_sem = [(new_sem(), new_sem()) for _ in range(2)]
    plane = [4 * lax.rem(z + kz, 4) + lax.rem(x + kx, 4) for kx, kz in FAR_FIRST]

    def shots_out(sweep):
        for k in (2, 1, 3):
            send(zs_st.at[sweep], zs_rv.at[sweep, y], *shots_sem[sweep], at_axis(1, lax.rem(y + k, 4)))
        zs_rv[sweep, y] = zs_st[sweep]

    def rcvs_out(sweep):
        for to in plane:
            rows = pl.ds(pl.multiple_of(to * 32, 32), 32)
            send(zr_st.at[sweep, rows], zr_rv.at[sweep, i], *rcvs_sem[sweep], (to, j))
        zr_rv[sweep, i] = zr_st[sweep, my_rcv]

    def shots_in(sweep):
        arrived(zs_rv.at[sweep, pl.ds(0, 3)], shots_sem[sweep][1])
        zs = zs_rv[sweep, 0].astype(F32)
        for k in range(1, 4):
            zs += zs_rv[sweep, k].astype(F32)
        shot_ph[sweep] = soft(zs)

    def rcvs_in(sweep):
        arrived(zr_rv.at[sweep, pl.ds(0, 15)], rcvs_sem[sweep][1])
        zr = zr_rv[sweep, 0].astype(F32)
        for k in range(1, 16):
            zr += zr_rv[sweep, k].astype(F32)
        return soft(zr)

    both = []
    for h in range(2):
        rows = slice(TR * h, TR * (h + 1))
        both.append(dot(member[h], high[rows]) )
        zr_st[0, RCV_DEV * h:RCV_DEV * (h + 1)] = both[h][SHOT_DEV:].astype(BF)
    zs_st[0] = (both[0][:SHOT_DEV] + both[1][:SHOT_DEV]).astype(BF)
    shots_out(0)
    rcvs_out(0)
    rcv_ph[0, my_rcv] = rcvs_in(0)
    ref = rcv_ph.at[0, my_rcv]
    for to in plane:
        send(ref, ref, *back_sem[0], (to, j))
    shots_in(0)

    def turned():
        @pl.loop(0, 8)
        def _(k):
            rows = pl.ds(pl.multiple_of(k * 128, 128), 128)
            put_high(rows, times_conj(groups(cross[rows]), groups(turn[rows]), low))

    turn[...] = dot(shot_one[...], shot_ph[0])
    turned()
    for h in range(2):
        rows = slice(TR * h, TR * (h + 1))
        m = member[h, SHOT_DEV:]
        zr_st[1, RCV_DEV * h:RCV_DEV * (h + 1)] = (dot(m, high[rows])).astype(BF)
    rcvs_out(1)
    arrived(rcv_ph.at[0, pl.ds(0, 480)], back_sem[0][1])
    for h in range(2):
        rows = slice(TR * h, TR * (h + 1))
        turn[rows] = dot(rcv_one[rows], rcv_ph[0, RCV_DEV * h:RCV_DEV * (h + 1)])
    turned()
    zs = []
    for h in range(2):
        rows = slice(TR * h, TR * (h + 1))
        m = member[h, :SHOT_DEV]
        zs.append(dot(m, high[rows]))
    zs_st[1] = (zs[0] + zs[1]).astype(BF)
    shots_out(1)

    rcv_ph[1, my_rcv] = rcvs_in(1)
    ref = rcv_ph.at[1, my_rcv]
    home = lax.div(i, 8)
    rows = pl.ds(pl.multiple_of(lax.rem(i, 8) * 32, 32), 32)
    for to in plane:
        send(ref, rcv_out.at[c, rows], *back_sem[1], (to, 2 * y + home))

    @pl.when(home == c)
    def _():
        rcv_out[c, rows] = rcv_ph[1, my_rcv]

    @pl.when(home != c)
    def _():
        send(ref, rcv_out.at[c, rows], *back_sem[1], partner)

    shots_in(1)
    last = send(shot_ph.at[1], shot_out.at[c], new_sem(), new_sem(), partner)
    shot_out[c] = shot_ph[1]
    sent(part.at[:, pl.ds(0, 3)], slabs_out)
    sent(dir2, level1_out)
    sent(last_in.at[:, pl.ds(0, 3)], last_out)
    sent(part.at[:, pl.ds(0, 3)], ag0_out)
    sent(dir2, ag1_out)
    for sweep in range(2):
        sent(zs_rv.at[sweep, pl.ds(0, 3)], shots_sem[sweep][0])
        sent(zr_rv.at[sweep, pl.ds(0, 15)], rcvs_sem[sweep][0])
    sent(rcv_ph.at[0, pl.ds(0, 480)], back_sem[0][0])
    last.wait()

    @pl.when(home == c)
    def _():
        sent(rcv_ph.at[1, pl.ds(0, 480)], back_sem[1][0])
        arrived(rcv_ph.at[1, pl.ds(0, 480)], back_sem[1][1])

    @pl.when(home != c)
    def _():
        sent(rcv_ph.at[1], back_sem[1][0])
        arrived(rcv_ph.at[1], back_sem[1][1])


def unpack(shots, rcvs, shot_out, rcv_out):
    for src, dst, n in ((shots, shot_out, SHOT_DEV), (rcvs, rcv_out, RCV_DEV)):
        mask = low_half(n)
        first, last = (groups(src[h].astype(F32)) for h in range(2))
        for part in range(2):
            dst[part, :, 0:128] = first[part]
            dst[part, :, 256:384] = last[part]
        dst[0, :, 128:256] = jnp.where(mask, first[2], swap(last[2]))
        dst[1, :, 128:256] = jnp.where(mask, swap(first[2]), last[2])


def shards(table, traces, cmp_bin, shot_index, rcv_index, live):
    vmem = pl.BlockSpec(memory_space=pltpu.VMEM)
    hbm = pl.BlockSpec(memory_space=pl.ANY)
    dma = pltpu.SemaphoreType.DMA
    packed = pl.pallas_call(
        kernel,
        out_shape=(
            jax.ShapeDtypeStruct((2, SHOT_DEV, HC), BF),
            jax.ShapeDtypeStruct((2, RCV_DEV, HC), BF),
        ),
        in_specs=[hbm] * 6,
        out_specs=(vmem, vmem),
        scratch_shapes=[
            pltpu.VMEM((NT, TR), BF),
            pltpu.VMEM((2, HC, NT), BF),
            pltpu.VMEM((4, 1, TR), jnp.int32),
            pltpu.VMEM((2, TR, HC), BF),
            pltpu.VMEM((TR, HC), BF),
            pltpu.VMEM((2, 8, TR), jnp.int32),
            pltpu.VMEM((NB, 2 * TR), BF),
            pltpu.VMEM((2 * TR, NB), BF),
            pltpu.VMEM((3, 4, 4, 4, 4, 16, 128), BF),
            pltpu.VMEM((3, 4, 4, 4, 4, 16, 128), BF),
            pltpu.VMEM((2 * TR, HC), F32),
            pltpu.VMEM((2 * TR, HC), F32),
            pltpu.VMEM((2 * TR, HC), BF),
            pltpu.VMEM((2, 8, 128), F32),
            pltpu.VMEM((2, SHOT_DEV + RCV_DEV, TR), BF),
            pltpu.VMEM((2 * TR, SHOT_DEV), BF),
            pltpu.VMEM((2 * TR, RCV_DEV), BF),
            pltpu.VMEM((2, SHOT_DEV, HC), BF),
            pltpu.VMEM((2, 2 * RCV_DEV, HC), BF),
            pltpu.VMEM((2, 4, SHOT_DEV, HC), BF),
            pltpu.VMEM((2, 16, 32, HC), BF),
            pltpu.VMEM((2, SHOT_DEV, HC), BF),
            pltpu.VMEM((2, 2 * RCV_DEV, HC), BF),
            pltpu.VMEM((3, 4, 4, 4, 16, 128), BF),
            pltpu.VMEM((3, 2, 4, 4, 4, 16, 128), BF),
            pltpu.VMEM((3, 3, 4, 4, 16, 128), BF),
            pltpu.VMEM((3, 4, 4, 4, 16, 128), BF),
            dma((112,)),
        ],
        compiler_params=pltpu.CompilerParams(
            collective_id=0, has_side_effects=True, vmem_limit_bytes=56 * 1024 * 1024
        ),
    )(traces.T, table, *(v.reshape(1, TR) for v in (cmp_bin, shot_index, rcv_index, live)))
    return pl.pallas_call(
        unpack,
        out_shape=(
            jax.ShapeDtypeStruct((2, SHOT_DEV, NF), F32),
            jax.ShapeDtypeStruct((2, RCV_DEV, NF), F32),
        ),
        in_specs=[vmem] * 2,
        out_specs=(vmem, vmem),
    )(*packed)


def solution(mesh):
    split = P(("shot", "rcv"))
    table = dft_halves()

    def run(traces, cmp_bin, shot_index, rcv_index, live):
        return jax.shard_map(
            shards,
            mesh=mesh,
            in_specs=(P(), P(("shot", "rcv"), None), split, split, split, split),
            out_specs=(P(None, "shot", None), P(None, "rcv", None)),
            check_vma=False,
        )(jnp.asarray(table), traces, cmp_bin, shot_index, rcv_index, live)

    return run
```

```python
import itertools
import math

import jax
import jax.numpy as jnp
import numpy as np
from jax import lax
from jax.experimental import pallas as pl
from jax.experimental.pallas import tpu as pltpu
from jax.sharding import PartitionSpec as P

NT = 2000
NF = 384
FLO = 20
SHOT_DEV = 128
RCV_DEV = 256
TR = 512
NB = 4096
HC = NF
MESH = pl.DeviceIdType.MESH
ORDER = ((0, 1, 2), (1, 2, 0), (2, 0, 1))
FAR_FIRST = ((2, 2), (3, 2), (2, 3), (2, 1), (1, 2), (3, 3), (3, 1), (2, 0), (1, 3), (1, 1), (0, 2), (3, 0), (1, 0), (0, 3), (0, 1))
BF = jnp.bfloat16
F32 = jnp.float32


def dft_halves():
    sample = np.arange(NT, dtype=np.int32)
    band = FLO + np.arange(NF, dtype=np.int32)
    angles = (band[:, None] * sample[None, :] % NT).astype(np.float32) * np.float32(2.0 * math.pi / NT)
    factor = np.float32(1.0 / math.sqrt(NT))
    re, im = np.cos(angles) * factor, -np.sin(angles) * factor
    halves = [np.concatenate([re[a:a + 128], im[a:a + 128], re[b:b + 64], im[b:b + 64]])
              for a, b in ((0, 128), (256, 192))]
    return np.stack(halves).astype(jnp.bfloat16)


def dot(a, b):
    return jnp.dot(a, b, preferred_element_type=F32)


def swap(v):
    return pltpu.roll(v, 64, axis=1)


def low_half(rows):
    return lax.broadcasted_iota(jnp.int32, (rows, 128), 1) < 64


def packed_conj(a, b, low):
    same = a * b
    mixed = a * swap(b)
    return jnp.where(low, same + swap(same), mixed - swap(mixed))


def times_conj(a, b, low):
    return a[0] * b[0] + a[1] * b[1], a[1] * b[0] - a[0] * b[1], packed_conj(a[2], b[2], low)


def soften(v):
    sq = [g * g for g in v]
    scale = lax.rsqrt(sq[0] + sq[1] + 1.0)
    return (v[0] * scale, v[1] * scale, v[2] * lax.rsqrt(sq[2] + swap(sq[2]) + 1.0))


def groups(v):
    return tuple(v[:, 128 * s:128 * (s + 1)] for s in range(3))


def kernel(traces_hbm, table_hbm, cmp_bin, shot_index, rcv_index, live, shot_out, rcv_out,
           traces, table, raw, spec, theirs, idxs, oh, oht, part, pilot, cross, turn, high, power, member, shot_one,
           rcv_one, zs_st, zr_st, zs_rv, zr_rv, shot_ph, rcv_ph, opp1, dir1, dir2, last_in, sems):
    i = lax.axis_index("shot")
    j = lax.axis_index("rcv")
    z, x = lax.div(i, 4), lax.rem(i, 4)
    y, c = lax.div(j, 2), lax.rem(j, 2)
    coord = (x, y, z)
    oc = 1 - c
    partner = (i, 2 * y + oc)
    numbers = itertools.count()

    def new_sem():
        return sems.at[next(numbers)]

    def at_axis(d, v):
        if d == 0:
            return (z * 4 + v, j)
        if d == 1:
            return (i, 2 * v + c)
        return (v * 4 + x, j)

    def fetch(src, dst, sem):
        copy = pltpu.make_async_copy(src, dst, sem)
        copy.start()
        return copy

    raw_sem, traces_sem = new_sem(), new_sem()
    for n, ref in enumerate((cmp_bin, shot_index, rcv_index, live)):
        fetch(ref, raw.at[n], raw_sem)
    for n in range(4):
        rows = pl.ds(512 * n, min(512, NT - 512 * n))
        fetch(traces_hbm.at[rows], traces.at[rows], traces_sem)
    table_in = [[fetch(table_hbm.at[h, pl.ds(128 * g, 128)], table.at[n, pl.ds(128 * g, 128)], new_sem())
                 for g in range(3)] for n, h in enumerate((oc, c))]

    barrier = pltpu.get_barrier_semaphore()
    for d in range(3):
        for k in (2, 1, 3):
            pl.semaphore_signal(barrier, inc=1, device_id=at_axis(d, lax.rem(coord[d] + k, 4)), device_id_type=MESH)
    pl.semaphore_signal(barrier, inc=1, device_id=partner, device_id_type=MESH)

    def send(src, dst, s_sem, r_sem, dev):
        copy = pltpu.make_async_remote_copy(src_ref=src, dst_ref=dst, send_sem=s_sem, recv_sem=r_sem, device_id=dev,
                                            device_id_type=MESH)
        copy.start()
        return copy

    def arrived(ref, sem):
        pltpu.make_async_remote_copy(src_ref=ref, dst_ref=ref, send_sem=sem, recv_sem=sem, device_id=partner,
                                     device_id_type=MESH).wait_recv()

    def sent(ref, sem):
        pltpu.make_async_remote_copy(src_ref=ref, dst_ref=ref, send_sem=sem, recv_sem=sem, device_id=partner,
                                     device_id_type=MESH).wait_send()

    pltpu.make_async_copy(raw, raw, raw_sem).wait()
    idxs[c, 0:1] = jnp.where(raw[3] != 0, raw[0], -1)
    idxs[c, 1:2] = raw[1] - i * SHOT_DEV
    idxs[c, 2:3] = raw[2] - j * RCV_DEV
    idxs[c, 3:8] = jnp.zeros((5, TR), jnp.int32)
    pltpu.make_async_copy(traces, traces, traces_sem).wait()

    def dft(n, dst):
        for g in range(3):
            table_in[n][g].wait()
            v = dot(table[n, 128 * g:128 * (g + 1)], traces[...])
            dst[:, 128 * g:128 * (g + 1)] = jnp.transpose(v).astype(BF)

    dft(0, theirs)
    pl.semaphore_wait(barrier, 10)
    idx_copy = send(idxs.at[c], idxs.at[c], new_sem(), new_sem(), partner)
    spec_copy = send(theirs, spec.at[c], new_sem(), new_sem(), partner)
    dft(1, spec.at[c])
    idx_copy.wait()

    bin_row = jnp.concatenate([idxs[0, 0:1, :], idxs[1, 0:1, :]], axis=1)

    @pl.loop(0, NB // 128)
    def _(k):
        bins = lax.broadcasted_iota(jnp.int32, (128, 2 * TR), 0) + k * 128
        oh[pl.ds(pl.multiple_of(k * 128, 128), 128)] = jnp.where(bins == bin_row, 1.0, 0.0).astype(BF)

    spec_copy.wait()

    def where(s, r, fixed):
        return (s, r) + tuple(fixed[d] if d in fixed else slice(None) for d in (2, 1, 0))

    def fixed_of(s, level):
        return {d: coord[d] for d in ORDER[s][:level]}

    def by_slab():
        return [[new_sem() for _ in range(4)] for _ in range(3)]

    slabs_out, level1_out, last_out = new_sem(), new_sem(), new_sem()
    far_in = [[new_sem() for _ in range(4)] for _ in range(3)]
    slabs_in, level1_in, last_sem = by_slab(), by_slab(), by_slab()

    def far_send(s, r):
        d = ORDER[s][0]
        near, far = lax.rem(coord[d] + (1 if r % 2 == 0 else 3), 4), lax.rem(coord[d] + 2, 4)
        send(part.at[where(s, r, {d: far})], opp1.at[s, r], slabs_out, far_in[s][r], at_axis(d, near))

    def away_send(s, r):
        d = ORDER[s][0]
        away = lax.rem(coord[d] + (3 if r % 2 == 0 else 1), 4)
        send(part.at[where(s, r, {d: away})], dir1.at[s, r % 2, r], slabs_out, slabs_in[s][r], at_axis(d, away))

    def slab_forward(s, r):
        d = ORDER[s][0]
        near = lax.rem(coord[d] + (1 if r % 2 == 0 else 3), 4)
        arrived(opp1.at[s, r], far_in[s][r])
        at = where(s, r, {d: near})
        part[at] = (part[at].astype(F32) + opp1[s, r].astype(F32)).astype(BF)
        send(part.at[at], dir1.at[s, 1 - r % 2, r], slabs_out, slabs_in[s][r], at_axis(d, near))

    def slab_finish(s, r):
        arrived(dir1.at[s, :, pl.ds(r, 1)], slabs_in[s][r])
        at = where(s, pl.ds(r, 1), fixed_of(s, 1))
        rows = pl.ds(r, 1)
        part[at] = (part[at].astype(F32) + dir1[s, 0, rows].astype(F32) + dir1[s, 1, rows].astype(F32)).astype(BF)
        d = ORDER[s][1]
        for k in (2, 1, 3):
            q = lax.rem(coord[d] + k, 4)
            src = part.at[where(s, rows, {**fixed_of(s, 1), d: q})]
            send(src, dir2.at[s, k - 1, rows], level1_out, level1_in[s][r], at_axis(d, q))

    def level1_finish(s, r):
        rows = pl.ds(r, 1)
        arrived(dir2.at[s, :, rows], level1_in[s][r])
        at = where(s, rows, fixed_of(s, 2))
        v = [dir2[s, k, rows].astype(F32) for k in range(3)]
        v = ((part[at].astype(F32) + v[0]) + (v[1] + v[2])).astype(BF)
        d = ORDER[s][2]
        last_in[s, coord[d], rows] = v
        for k in (2, 1, 3):
            ref = last_in.at[s, coord[d], rows]
            send(ref, ref, last_out, last_sem[s][r], at_axis(d, lax.rem(coord[d] + k, 4)))

    def last_finish(s, r):
        rows = pl.ds(r, 1)
        arrived(last_in.at[s, pl.ds(0, 3), rows], last_sem[s][r])
        v = [last_in[s, k, rows].astype(F32) for k in range(4)]
        pilot[where(s, rows, fixed_of(s, 2))] = ((v[0] + v[1]) + (v[2] + v[3])).astype(BF)

    for r in range(4):
        v = dot(oh[1024 * r:1024 * (r + 1)], spec[...].reshape(2 * TR, HC)).astype(BF)
        for s in range(3):
            part[s, r] = v[:, 128 * s:128 * (s + 1)].reshape(4, 4, 4, 16, 128)
        for s in range(3):
            far_send(s, r)
        for s in range(3):
            away_send(s, r)

    lane = lax.broadcasted_iota(jnp.int32, (128, 128), 1)

    def other_one_hot(n):
        @pl.loop(2 * n, 2 * n + 2)
        def _(k):
            half = lax.div(k, 4)
            lanes = pl.ds(pl.multiple_of(lax.rem(k, 4) * 128, 128), 128)
            rows = pl.ds(pl.multiple_of(k * 128, 128), 128)
            col = jnp.transpose(jnp.broadcast_to(idxs[half, 0:1, lanes], (128, 128)))
            for n in range(NB // 128):
                oht[rows, 128 * n:128 * (n + 1)] = jnp.where(col == lane + 128 * n, 1.0, 0.0).astype(BF)
            col = jnp.transpose(jnp.broadcast_to(idxs[half, 1:2, lanes], (128, 128)))
            shot_one[rows] = jnp.where(col == lane, 1.0, 0.0).astype(BF)
            col = jnp.transpose(jnp.broadcast_to(idxs[half, 2:3, lanes], (128, 128)))
            for n in range(2):
                rcv_one[rows, 128 * n:128 * (n + 1)] = jnp.where(col == lane + 128 * n, 1.0, 0.0).astype(BF)

    for h in range(2):
        shots = lax.broadcasted_iota(jnp.int32, (SHOT_DEV, TR), 0)
        member[h, :SHOT_DEV] = jnp.where(shots == idxs[h, 1:2, :], 1.0, 0.0).astype(BF)
        rcvs = lax.broadcasted_iota(jnp.int32, (RCV_DEV, TR), 0)
        member[h, SHOT_DEV:] = jnp.where(rcvs == idxs[h, 2:3, :], 1.0, 0.0).astype(BF)

    ag0_out, ag1_out = new_sem(), new_sem()
    ag1_in = by_slab()
    ag_far = [[new_sem() for _ in range(4)] for _ in range(3)]
    ag_in = [new_sem() for _ in range(4)]

    def ag_slab(s, r, way):
        d = ORDER[s][0]
        ref = pilot.at[where(s, r, fixed_of(s, 1))]
        sem = ag_far[s][r] if way == r % 2 else ag_in[r]
        send(ref, ref, ag0_out, sem, at_axis(d, lax.rem(coord[d] + (1, 3)[way], 4)))

    def ag_forward(s, r):
        d = ORDER[s][0]
        way = r % 2
        ref = pilot.at[where(s, r, {d: lax.rem(coord[d] + (3, 1)[way], 4)})]
        arrived(ref, ag_far[s][r])
        send(ref, ref, ag0_out, ag_in[r], at_axis(d, lax.rem(coord[d] + (1, 3)[way], 4)))

    def gather_send(s, r):
        last_finish(s, r)
        d = ORDER[s][1]
        ref = pilot.at[where(s, pl.ds(r, 1), fixed_of(s, 2))]
        for k in (2, 1, 3):
            send(ref, ref, ag1_out, ag1_in[s][r], at_axis(d, lax.rem(coord[d] + k, 4)))

    def gather_slab(s, r):
        arrived(dir2.at[s, :, pl.ds(r, 1)], ag1_in[s][r])
        ag_slab(s, r, r % 2)
        ag_slab(s, r, 1 - r % 2)

    for n, step in enumerate((slab_forward, slab_finish, level1_finish, gather_send, gather_slab, ag_forward)):
        if n > 1:
            other_one_hot(n - 2)
        for r in range(4):
            for s in range(3):
                step(s, r)

    for r in range(4):
        arrived(part.at[:, 0, pl.ds(0, 2)], ag_in[r])
        v = dot(oht[:, 1024 * r:1024 * (r + 1)],
                jnp.concatenate([pilot[s, r].reshape(1024, 128) for s in range(3)], axis=1))
        if r == 0:
            cross[...] = v
        else:
            cross[...] += v

    low = low_half(128)

    @pl.loop(0, 8)
    def _(k):
        v = groups(cross[pl.ds(pl.multiple_of(k * 128, 128), 128)])
        p = jnp.sum(v[0] * v[0] + v[1] * v[1] + v[2] * v[2], axis=1, keepdims=True)
        power[c, pl.ds(k, 1)] = jnp.transpose(jnp.broadcast_to(p, (128, 128)))[0:1]

    p_copy = send(power.at[c], power.at[c], new_sem(), new_sem(), partner)

    @pl.loop(0, 8)
    def _(k):
        rows = pl.ds(pl.multiple_of(k * 128, 128), 128)
        inner = pl.ds(pl.multiple_of(lax.rem(k, 4) * 128, 128), 128)
        v = times_conj(groups(spec[lax.div(k, 4), inner].astype(F32)), groups(cross[rows]), low)
        for s in range(3):
            cross[rows, 128 * s:128 * (s + 1)] = v[s]

    def put_high(rows, v):
        for s in range(3):
            high[rows, 128 * s:128 * (s + 1)] = v[s].astype(BF)

    p_copy.wait()

    @pl.loop(0, 8)
    def _(k):
        rows = pl.ds(pl.multiple_of(k * 128, 128), 128)
        p = power[0, pl.ds(k, 1)] + power[1, pl.ds(k, 1)]
        scale = lax.rsqrt(jnp.transpose(jnp.broadcast_to(p, (128, 128))) / NF + 1e-06)
        v = [g * scale for g in groups(cross[rows])]
        for s in range(3):
            cross[rows, 128 * s:128 * (s + 1)] = v[s]
        put_high(rows, v)

    def soft(v):
        return jnp.concatenate(soften(groups(v)), axis=1).astype(BF)

    my_rcv = pl.ds(pl.multiple_of(i * 32, 32), 32)
    shots_sem = [(new_sem(), new_sem()) for _ in range(2)]
    rcvs_sem = [(new_sem(), new_sem()) for _ in range(2)]
    back_sem = [(new_sem(), new_sem()) for _ in range(2)]
    plane = [4 * lax.rem(z + kz, 4) + lax.rem(x + kx, 4) for kx, kz in FAR_FIRST]

    def shots_out(sweep):
        for k in (2, 1, 3):
            send(zs_st.at[sweep], zs_rv.at[sweep, y], *shots_sem[sweep], at_axis(1, lax.rem(y + k, 4)))
        zs_rv[sweep, y] = zs_st[sweep]

    def rcvs_out(sweep):
        for to in plane:
            rows = pl.ds(pl.multiple_of(to * 32, 32), 32)
            send(zr_st.at[sweep, rows], zr_rv.at[sweep, i], *rcvs_sem[sweep], (to, j))
        zr_rv[sweep, i] = zr_st[sweep, my_rcv]

    def shots_in(sweep):
        arrived(zs_rv.at[sweep, pl.ds(0, 3)], shots_sem[sweep][1])
        zs = zs_rv[sweep, 0].astype(F32)
        for k in range(1, 4):
            zs += zs_rv[sweep, k].astype(F32)
        shot_ph[sweep] = soft(zs)

    def rcvs_in(sweep):
        arrived(zr_rv.at[sweep, pl.ds(0, 15)], rcvs_sem[sweep][1])
        zr = zr_rv[sweep, 0].astype(F32)
        for k in range(1, 16):
            zr += zr_rv[sweep, k].astype(F32)
        return soft(zr)

    both = []
    for h in range(2):
        rows = slice(TR * h, TR * (h + 1))
        both.append(dot(member[h], high[rows]) )
        zr_st[0, RCV_DEV * h:RCV_DEV * (h + 1)] = both[h][SHOT_DEV:].astype(BF)
    zs_st[0] = (both[0][:SHOT_DEV] + both[1][:SHOT_DEV]).astype(BF)
    shots_out(0)
    rcvs_out(0)
    rcv_ph[0, my_rcv] = rcvs_in(0)
    ref = rcv_ph.at[0, my_rcv]
    for to in plane:
        send(ref, ref, *back_sem[0], (to, j))
    shots_in(0)

    def turned():
        @pl.loop(0, 8)
        def _(k):
            rows = pl.ds(pl.multiple_of(k * 128, 128), 128)
            put_high(rows, times_conj(groups(cross[rows]), groups(turn[rows]), low))

    turn[...] = dot(shot_one[...], shot_ph[0])
    turned()
    for h in range(2):
        rows = slice(TR * h, TR * (h + 1))
        m = member[h, SHOT_DEV:]
        zr_st[1, RCV_DEV * h:RCV_DEV * (h + 1)] = (dot(m, high[rows])).astype(BF)
    rcvs_out(1)
    arrived(rcv_ph.at[0, pl.ds(0, 480)], back_sem[0][1])
    for first, number in ((0, 256), (256, 128)):
        lanes = slice(first, first + number)
        for h in range(2):
            rows = slice(TR * h, TR * (h + 1))
            turn[rows, lanes] = dot(rcv_one[rows], rcv_ph[0, RCV_DEV * h:RCV_DEV * (h + 1), lanes])

        @pl.loop(0, 8)
        def _(k):
            rows = pl.ds(pl.multiple_of(k * 128, 128), 128)
            if first == 0:
                a, b = [(v[rows, 0:128], v[rows, 128:256]) for v in (cross, turn)]
                high[rows, 0:128] = (a[0] * b[0] + a[1] * b[1]).astype(BF)
                high[rows, 128:256] = (a[1] * b[0] - a[0] * b[1]).astype(BF)
            else:
                high[rows, lanes] = packed_conj(cross[rows, lanes], turn[rows, lanes], low).astype(BF)

        zs = [dot(member[h, :SHOT_DEV], high[TR * h:TR * (h + 1), lanes]) for h in range(2)]
        zs_st[1, :, lanes] = (zs[0] + zs[1]).astype(BF)
        for k in (2, 1, 3):
            send(zs_st.at[1, :, pl.ds(first, number)], zs_rv.at[1, y, :, pl.ds(first, number)], *shots_sem[1],
                 at_axis(1, lax.rem(y + k, 4)))
    zs_rv[1, y] = zs_st[1]

    rcv_ph[1, my_rcv] = rcvs_in(1)
    ref = rcv_ph.at[1, my_rcv]
    home = lax.div(i, 8)
    rows = pl.ds(pl.multiple_of(lax.rem(i, 8) * 32, 32), 32)
    for to in plane:
        send(ref, rcv_out.at[c, rows], *back_sem[1], (to, 2 * y + home))

    @pl.when(home == c)
    def _():
        rcv_out[c, rows] = rcv_ph[1, my_rcv]

    @pl.when(home != c)
    def _():
        send(ref, rcv_out.at[c, rows], *back_sem[1], partner)

    shots_in(1)
    last = send(shot_ph.at[1], shot_out.at[c], new_sem(), new_sem(), partner)
    shot_out[c] = shot_ph[1]
    sent(part.at[:, pl.ds(0, 3)], slabs_out)
    sent(dir2, level1_out)
    sent(last_in.at[:, pl.ds(0, 3)], last_out)
    sent(part.at[:, pl.ds(0, 3)], ag0_out)
    sent(dir2, ag1_out)
    for sweep in range(2):
        sent(zs_rv.at[sweep, pl.ds(0, 3)], shots_sem[sweep][0])
        sent(zr_rv.at[sweep, pl.ds(0, 15)], rcvs_sem[sweep][0])
    sent(rcv_ph.at[0, pl.ds(0, 480)], back_sem[0][0])
    last.wait()

    @pl.when(home == c)
    def _():
        sent(rcv_ph.at[1, pl.ds(0, 480)], back_sem[1][0])
        arrived(rcv_ph.at[1, pl.ds(0, 480)], back_sem[1][1])

    @pl.when(home != c)
    def _():
        sent(rcv_ph.at[1], back_sem[1][0])
        arrived(rcv_ph.at[1], back_sem[1][1])


def unpack(shots, rcvs, shot_out, rcv_out):
    for src, dst, n in ((shots, shot_out, SHOT_DEV), (rcvs, rcv_out, RCV_DEV)):
        mask = low_half(n)
        first, last = (groups(src[h].astype(F32)) for h in range(2))
        for part in range(2):
            dst[part, :, 0:128] = first[part]
            dst[part, :, 256:384] = last[part]
        dst[0, :, 128:256] = jnp.where(mask, first[2], swap(last[2]))
        dst[1, :, 128:256] = jnp.where(mask, swap(first[2]), last[2])


def shards(table, traces, cmp_bin, shot_index, rcv_index, live):
    vmem = pl.BlockSpec(memory_space=pltpu.VMEM)
    hbm = pl.BlockSpec(memory_space=pl.ANY)
    dma = pltpu.SemaphoreType.DMA
    packed = pl.pallas_call(
        kernel,
        out_shape=(
            jax.ShapeDtypeStruct((2, SHOT_DEV, HC), BF),
            jax.ShapeDtypeStruct((2, RCV_DEV, HC), BF),
        ),
        in_specs=[hbm] * 6,
        out_specs=(vmem, vmem),
        scratch_shapes=[
            pltpu.VMEM((NT, TR), BF),
            pltpu.VMEM((2, HC, NT), BF),
            pltpu.VMEM((4, 1, TR), jnp.int32),
            pltpu.VMEM((2, TR, HC), BF),
            pltpu.VMEM((TR, HC), BF),
            pltpu.VMEM((2, 8, TR), jnp.int32),
            pltpu.VMEM((NB, 2 * TR), BF),
            pltpu.VMEM((2 * TR, NB), BF),
            pltpu.VMEM((3, 4, 4, 4, 4, 16, 128), BF),
            pltpu.VMEM((3, 4, 4, 4, 4, 16, 128), BF),
            pltpu.VMEM((2 * TR, HC), F32),
            pltpu.VMEM((2 * TR, HC), F32),
            pltpu.VMEM((2 * TR, HC), BF),
            pltpu.VMEM((2, 8, 128), F32),
            pltpu.VMEM((2, SHOT_DEV + RCV_DEV, TR), BF),
            pltpu.VMEM((2 * TR, SHOT_DEV), BF),
            pltpu.VMEM((2 * TR, RCV_DEV), BF),
            pltpu.VMEM((2, SHOT_DEV, HC), BF),
            pltpu.VMEM((2, 2 * RCV_DEV, HC), BF),
            pltpu.VMEM((2, 4, SHOT_DEV, HC), BF),
            pltpu.VMEM((2, 16, 32, HC), BF),
            pltpu.VMEM((2, SHOT_DEV, HC), BF),
            pltpu.VMEM((2, 2 * RCV_DEV, HC), BF),
            pltpu.VMEM((3, 4, 4, 4, 16, 128), BF),
            pltpu.VMEM((3, 2, 4, 4, 4, 16, 128), BF),
            pltpu.VMEM((3, 3, 4, 4, 16, 128), BF),
            pltpu.VMEM((3, 4, 4, 4, 16, 128), BF),
            dma((112,)),
        ],
        compiler_params=pltpu.CompilerParams(
            collective_id=0, has_side_effects=True, vmem_limit_bytes=56 * 1024 * 1024
        ),
    )(traces.T, table, *(v.reshape(1, TR) for v in (cmp_bin, shot_index, rcv_index, live)))
    return pl.pallas_call(
        unpack,
        out_shape=(
            jax.ShapeDtypeStruct((2, SHOT_DEV, NF), F32),
            jax.ShapeDtypeStruct((2, RCV_DEV, NF), F32),
        ),
        in_specs=[vmem] * 2,
        out_specs=(vmem, vmem),
    )(*packed)


def solution(mesh):
    split = P(("shot", "rcv"))
    table = dft_halves()

    def run(traces, cmp_bin, shot_index, rcv_index, live):
        return jax.shard_map(
            shards,
            mesh=mesh,
            in_specs=(P(), P(("shot", "rcv"), None), split, split, split, split),
            out_specs=(P(None, "shot", None), P(None, "rcv", None)),
            check_vma=False,
        )(jnp.asarray(table), traces, cmp_bin, shot_index, rcv_index, live)

    return run
```
